128 devices in a mesh: gx: 8 (over x, core), gy: 16 (over z, y).
Axes of the slice: x: 4, y: 4, z: 4, core: 2. Of those that a mesh axis runs over, the one named last changes fastest.
Arguments:
- rock_type: int32 [128, 512, 512], P('gx', 'gy'), may hold values from 0 to 7
- rock_perm: float32 [8], replicated, may hold values from 0.05 to 0.5
- rock_poro: float32 [8], replicated, may hold values from 0.1 to 0.35
- base_flux: float32 [128, 512, 512], P('gx', 'gy'), may hold values from 0.5 to 2
- initial_pressure: float32 [128, 512, 512], P('gx', 'gy'), may hold values from -6 to 6
- old_saturation: float32 [128, 512, 512], P('gx', 'gy'), may hold values from 0 to 1
- well_cells: int32 [3, 512], replicated, may hold values from 0 to 511, as said below
- well_rates: float32 [512], replicated, may hold values from -2 to 2
Outputs:
- pressure: float32 [128, 512, 512], P('gx', 'gy')
- saturation: float32 [128, 512, 512], P('gx', 'gy')
The draws below stay inside these ranges and needn't reach their ends.
Inputs may be any that keep to these rules, and one draw needn't show every extreme that they name: `well_cells`: row 0 holds first coordinates below 128, row 1 second coordinates below 512, row 2 third coordinates below 512. The first well lies in the last cell of the grid and the second in the first cell; wells may share a cell.
All inputs are finite; a program needn't handle non-finite values.
Results may differ from the reference program's by a relative error of at most 0.0003.
Values sent between devices are 32-bit elements; how exact they have to be, the bound alone decides.
A program may use at most 64 MiB of HBM per device.

```python
import math
import jax
import jax.numpy as jnp
from jax import lax

PASSES = 4
NEWTON = 3
ROCKS = 8
NX = 128
NY = 512
NZ = 512
WELLS = 512


def draw_well_cells(key, part):
    first_key, second_key, third_key = jax.random.split(jax.random.fold_in(key, 17), 3)
    coord_x = jax.random.randint(first_key, (WELLS,), 0, NX)
    coord_y = jax.random.randint(second_key, (WELLS,), 0, NY)
    coord_z = jax.random.randint(third_key, (WELLS,), 0, NZ)
    coord_x = coord_x.at[0].set(NX - 1).at[1].set(0)
    coord_y = coord_y.at[0].set(NY - 1).at[1].set(0)
    coord_z = coord_z.at[0].set(NZ - 1).at[1].set(0)
    return jnp.stack([coord_x, coord_y, coord_z]).astype(jnp.int32)


def place_ends(array, rng, smallest, high):
    shape = array.shape
    index_at = [jax.random.randint(jax.random.fold_in(rng, axis), (), 0, shape[axis]) for axis in range(len(shape))]
    array = array.at[tuple(index_at)].set(smallest)
    longest = shape.index(max(shape))
    index_at[longest] = (index_at[longest] + 1) % shape[longest]
    return array.at[tuple(index_at)].set(high)


def steps_of(rng, shape, cuts, smallest, high):
    gain = 1.0
    for dim, shards_of in cuts:
        heights = jax.random.uniform(jax.random.fold_in(jax.random.fold_in(rng, 6), dim), (shards_of,), jnp.float32, smallest / len(cuts), high / len(cuts))
        gain = gain * jnp.repeat(jnp.exp(heights), shape[dim] // shards_of).reshape((-1,) + (1,) * (len(shape) - 1 - dim))
    return gain


def noise(stream_key, dims, scale, most, shards=(), kind=jnp.bfloat16):
    entries = scale * jax.random.normal(stream_key, dims, jnp.float32)
    if shards:
        entries = entries * steps_of(stream_key, dims, shards, -0.22, 0.18)
    return jnp.clip(entries, -most, most).astype(kind)


def setup_inputs(seed: int = 0) -> dict:
    keys = jax.random.split(jax.random.key(seed), 9)
    rock_type = place_ends(jax.random.randint(keys[0], (NX, NY, NZ), 0, ROCKS), jax.random.fold_in(keys[0], 1), 0, ROCKS - 1).astype(jnp.int32)
    rock_perm = jnp.clip(jnp.exp(jax.random.uniform(keys[1], (ROCKS,), jnp.float32, math.log(0.05), math.log(0.5))), 0.05, 0.5)
    rock_poro = jnp.clip(jax.random.uniform(keys[2], (ROCKS,), jnp.float32, 0.1, 0.35), 0.1, 0.35)
    base_flux = jnp.clip(jnp.exp(math.log(2.0) - 1.3862944 * jax.random.uniform(keys[3], (NX, NY, NZ), jnp.float32) ** steps_of(keys[3], (NX, NY, NZ), ((0, 8), (1, 16)), -0.2, 0.2)), 0.5, 2.0)
    initial_pressure = noise(keys[4], (NX, NY, NZ), 1.0, 6.0, ((0, 8), (1, 16)), jnp.float32)
    old_saturation = jnp.clip(1.0 * jax.random.uniform(keys[5], (NX, NY, NZ), jnp.float32) ** steps_of(keys[5], (NX, NY, NZ), ((0, 8), (1, 16)), -0.2, 0.2), 0.0, 1.0)
    well_cells = draw_well_cells(jax.random.fold_in(keys[8], 71), 0)
    well_rates = jnp.clip(jax.random.uniform(keys[7], (WELLS,), jnp.float32, -2.0, 2.0), -2.0, 2.0)
    return dict(rock_type=rock_type, rock_perm=rock_perm, rock_poro=rock_poro, base_flux=base_flux, initial_pressure=initial_pressure, old_saturation=old_saturation, well_cells=well_cells, well_rates=well_rates)


MOBILITY = 0.5
OMEGA = 0.8
VOLUME = 4.0
COMPRESS = 0.5


def fraction(water):
    denom = water * water + MOBILITY * (1.0 - water) ** 2
    return water * water / denom


def fraction_slope(water):
    denom = water * water + MOBILITY * (1.0 - water) ** 2
    return 2.0 * MOBILITY * water * (1.0 - water) / (denom * denom)


def transmit(left, right):
    total = left + right
    return 2.0 * left * right / jnp.where(total > 0, total, 1.0)


def along_depth(field):
    deeper = jnp.pad(field[:, :, 1:], ((0, 0), (0, 0), (0, 1)))
    shallower = jnp.pad(field[:, :, :-1], ((0, 0), (0, 0), (1, 0)))
    return deeper, shallower


def links(perm_ext):
    center = perm_ext[1:-1, 1:-1]
    deeper, shallower = along_depth(center)
    return (transmit(center, perm_ext[2:, 1:-1]), transmit(center, perm_ext[:-2, 1:-1]),
            transmit(center, perm_ext[1:-1, 2:]), transmit(center, perm_ext[1:-1, :-2]),
            transmit(center, deeper), transmit(center, shallower))


def jacobi(press_ext, perm_ext, storage, source):
    east, west, north, south, below, above = links(perm_ext)
    center = press_ext[1:-1, 1:-1]
    deeper, shallower = along_depth(center)
    flow = (east * (center - press_ext[2:, 1:-1]) + west * (center - press_ext[:-2, 1:-1])
            + north * (center - press_ext[1:-1, 2:]) + south * (center - press_ext[1:-1, :-2])
            + below * (center - deeper) + above * (center - shallower))
    outside = jnp.where(perm_ext[1:-1, 1:-1] > 0, 0.0, 1.0)
    diagonal = storage + east + west + north + south + below + above + outside
    return center + OMEGA * (source - storage * center - flow) / diagonal


def upwind(flux, own, other):
    return jnp.maximum(flux, 0.0) * own + jnp.minimum(flux, 0.0) * other


def water_terms(press_ext, perm_ext, frac_old, frac_side, base_flux, rates_field):
    east, west, north, south, below, above = links(perm_ext)
    center = press_ext[1:-1, 1:-1]
    deeper, shallower = along_depth(center)
    frac_deep, frac_shallow = along_depth(frac_old)
    through = jnp.maximum(base_flux + east * (center - press_ext[2:, 1:-1]), 0.0)
    leaving = (upwind(north * (center - press_ext[1:-1, 2:]), frac_old, frac_side[:, 2:])
               + upwind(south * (center - press_ext[1:-1, :-2]), frac_old, frac_side[:, :-2])
               + upwind(below * (center - deeper), frac_old, frac_deep)
               + upwind(above * (center - shallower), frac_old, frac_shallow))
    explicit = jnp.maximum(rates_field, 0.0) + jnp.minimum(rates_field, 0.0) * frac_old - leaving
    return through, explicit


def sweep(inflow, volume, through, explicit, old_sat):
    def advance(incoming, items):
        vol_row, flux_row, extra_row, start_row = items
        water = start_row
        for _ in range(NEWTON):
            misfit = vol_row * (water - start_row) + flux_row * fraction(water) - incoming - extra_row
            water = jnp.clip(water - misfit / (vol_row + flux_row * fraction_slope(water)), 0.0, 1.0)
        return flux_row * fraction(water), water

    outgoing, saturation = lax.scan(advance, inflow, (volume, through, explicit, old_sat))
    return saturation, outgoing


def lookup(rock_type, table):
    result = jnp.zeros(rock_type.shape, table.dtype)
    for kind in range(table.shape[0]):
        result = jnp.where(rock_type == kind, table[kind], result)
    return result


def well_field(well_cells, well_rates, shape, anchor_x, anchor_y):
    local_x = well_cells[0] - anchor_x
    local_y = well_cells[1] - anchor_y
    local_z = well_cells[2]
    inside = (local_x >= 0) & (local_x < shape[0]) & (local_y >= 0) & (local_y < shape[1]) & (local_z >= 0) & (local_z < shape[2])
    count = shape[0] * shape[1] * shape[2]
    flat = jnp.where(inside, (local_x * shape[1] + local_y) * shape[2] + local_z, count).astype(jnp.int32)
    return jnp.zeros((count,), well_rates.dtype).at[flat].add(well_rates, mode="drop").reshape(shape)


def widen(field):
    return jnp.pad(field, ((1, 1), (1, 1), (0, 0)))


def reference(rock_type, rock_perm, rock_poro, base_flux, initial_pressure, old_saturation, well_cells, well_rates):
    perm = lookup(rock_type, rock_perm)
    volume = VOLUME * lookup(rock_type, rock_poro)
    storage = COMPRESS * volume
    rates_field = well_field(well_cells, well_rates, rock_type.shape, 0, 0)
    source = storage * initial_pressure + rates_field
    perm_ext = widen(perm)
    pressure = initial_pressure
    for _ in range(PASSES):
        pressure = jacobi(widen(pressure), perm_ext, storage, source)
    frac_old = fraction(old_saturation)
    frac_side = jnp.pad(frac_old, ((0, 0), (1, 1), (0, 0)))
    through, explicit = water_terms(widen(pressure), perm_ext, frac_old, frac_side, base_flux, rates_field)
    saturation, _ = sweep(base_flux[0], volume, through, explicit, old_saturation)
    return pressure, saturation
```

```python
import functools

import jax
import jax.numpy as jnp
from jax import lax
from jax.experimental import pallas as pl
from jax.experimental.pallas import tpu as pltpu
from jax.sharding import PartitionSpec as P

PASSES = 4
MOBILITY = 0.5
OMEGA = 0.8
VOLUME = 4.0
COMPRESS = 0.5

MESH = pl.DeviceIdType.MESH
LX = 16
NL = 32
EL = 41
LO = 4
ER = 40
RO = 12
ROCKS = 8
FAR = 1e30
NXC = 4
NGY = 16
WELLS = 512


def roll(value, shift):
    return pltpu.roll(value, shift % 128, 1)


def next_z(tiles):
    return [tiles[1], tiles[2], tiles[3], roll(tiles[0], -1)]


def prev_z(tiles):
    return [roll(tiles[3], 1), tiles[0], tiles[1], tiles[2]]


def layers(start, stop, block, body):
    whole = (stop - start) // block

    def several(i, _):
        for j in range(block):
            body(start + block * i + j)
        return 0

    lax.fori_loop(0, whole, several, 0)
    for l in range(start + block * whole, stop):
        body(l)


def recip(value):
    return pl.reciprocal(value, approx=False)


def permuted(value, matrix, parts):
    total, rest = None, value
    for k in range(parts):
        piece = rest.astype(jnp.bfloat16)
        term = jnp.dot(piece, matrix, preferred_element_type=jnp.float32)
        total = term if total is None else total + term
        if k < parts - 1:
            rest = rest - piece.astype(jnp.float32)
    return total


def lanes(z):
    return slice(128 * z, 128 * z + 128)


def step_kernel(
    rock, perm_tab, poro_tab, base, press, sat0, wells, well_rates,
    out_p, out_s,
    st_r, st_p, st_s, st_b,
    in_r, in_p, in_s, in_b, my_r, my_p, my_s, my_b, pk_r, pk_p, pk_s, pk_c, ys_r, ys_p, ys_s, co,
    hh, st, pa, pb, te, tn, tb, ww, src, rt, hot_a, hot_b, fs, order, back,
    face_in, face_out, res_p, res_s,
    loc, snd, rcv,
):
    gx, gy = lax.axis_index("gx"), lax.axis_index("gy")
    xc, core = gx // 2, lax.rem(gx, 2)
    partner = (gx + 1 - 2 * core, gy)
    low, high = xc > 0, xc < NXC - 1
    down, up = gy > 0, gy < NGY - 1
    f32 = jnp.float32

    barrier = pltpu.get_barrier_semaphore()
    count = jnp.int32(0)
    for dx in (-1, 0, 1):
        for dy in (-1, 0, 1):
            for other in (0, 1):
                there = (xc + dx >= 0) & (xc + dx < NXC) & (gy + dy >= 0) & (gy + dy < NGY)
                if dx == 0 and dy == 0:
                    there = there & (core != other)
                count = count + there.astype(jnp.int32)

                @pl.when(there)
                def _(dx=dx, dy=dy, other=other):
                    pl.semaphore_signal(
                        barrier, inc=1, device_id=(2 * (xc + dx) + other, gy + dy), device_id_type=MESH
                    )

    def local(k, a, b):
        return pltpu.make_async_copy(a, b, loc.at[k])

    row24 = pl.ds(pl.multiple_of(8 * core, 8), 24)
    row16 = pl.ds(pl.multiple_of(16 * core, 16), 16)
    own = pl.ds(LO + LX * core, LX)
    own0 = pl.ds(LX * core, LX)
    loads = [
        local(0, rock, in_r), local(1, press, in_p), local(2, sat0, in_s), local(3, base, in_b)
    ]
    for copy in loads:
        copy.start()
    blocks = [
        local(4, my_r.at[:, row24, :], st_r.at[own]),
        local(5, my_p.at[:, row24, :], st_p.at[own]),
        local(6, my_s.at[:, row24, :], st_s.at[own0]),
        local(7, my_b.at[:, row16, :], st_b.at[own0]),
    ]

    def remote(k, j, a, b, device):
        return pltpu.make_async_remote_copy(
            src_ref=a, dst_ref=b, send_sem=snd.at[k], recv_sem=rcv.at[j], device_id=device, device_id_type=MESH
        )

    other24 = pl.ds(pl.multiple_of(8 * (1 - core), 8), 24)
    other16 = pl.ds(pl.multiple_of(16 * (1 - core), 16), 16)
    sends = []
    ypart = pl.ds(pl.multiple_of(LX * core, 16), LX)
    last_layers, first_layers = (core == 1) & high, (core == 0) & low
    for k, (a, b, pk, ys) in enumerate(((my_r, st_r, pk_r, ys_r), (my_p, st_p, pk_p, ys_p))):
        for side, ok, device in ((0, down, (2 * xc + 1, gy - 1)), (1, up, (2 * xc, gy + 1))):
            sends.append((ok, remote(4 + 2 * k + side, 4 + k, pk.at[side], ys.at[:, ypart, :], device)))
        for d in (0, 1):
            rows, place = pl.ds(16 * d, 16), pl.ds(8 * d, 16)
            sends.append((last_layers, remote(
                8 + 2 * d + k, 7 + k, a.at[pl.ds(12, 4), rows, :], b.at[pl.ds(0, 4), place, :], (2 * (xc + 1) + d, gy),
            )))
            sends.append((first_layers, remote(
                8 + 2 * d + k, 9 + k, a.at[pl.ds(0, 5), rows, :], b.at[pl.ds(LO + NL, 5), place, :], (2 * (xc - 1) + d, gy),
            )))
        sends.append((None, remote(k, k, a.at[:, other24, :], b.at[own], partner)))
    for group, (ok, d, dy, kind) in enumerate(((down, 1, -1, 0), (up, 0, 1, 0), (None, 1, 0, 1), (None, 0, 0, 1))):
        for part, side, dx in ((last_layers, 0, 1), (first_layers, 1, -1)):
            sends.append((
                part if ok is None else part & ok,
                remote(12 + group, 11 + 2 * kind + side, pk_c.at[group], co.at[kind, side], (2 * (xc + dx) + d, gy + dy)),
            ))
    sends_late = []
    for side, ok, device in ((0, down, (2 * xc + 1, gy - 1)), (1, up, (2 * xc, gy + 1))):
        sends_late.append((ok, remote(16 + side, 6, pk_s.at[side], ys_s.at[ypart, :], device)))
    sends_late.append((None, remote(2, 2, my_s.at[:, other24, :], st_s.at[own0], partner)))
    sends_late.append((None, remote(3, 3, my_b.at[:, other16, :], st_b.at[own0], partner)))

    def guarded(ok, action):
        if ok is None:
            action()
        else:
            pl.when(ok)(action)

    def arrived(k, ref, ok=None):
        guarded(ok, lambda: pltpu.make_async_copy(ref, ref, rcv.at[k]).wait())

    outer = ((core == 0) & down) | ((core == 1) & up)

    def depth_of(place):
        return 4 * lax.rem(place, 128) + place // 128

    ahead = lax.broadcasted_iota(jnp.int32, (512, 512), 0)
    aside = lax.broadcasted_iota(jnp.int32, (512, 512), 1)
    order[...] = jnp.where(ahead == depth_of(aside), 1.0, 0.0).astype(jnp.bfloat16)
    back[...] = jnp.where(depth_of(ahead) == aside, 1.0, 0.0).astype(jnp.bfloat16)

    def reorder(a, b, parts):
        def body(m, _):
            at = pl.ds(pl.multiple_of(8 * m, 8), 8)
            value = a[at].reshape(256, 512).astype(f32)
            b[at] = permuted(value, order[...], parts).reshape(8, 32, 512)
            return 0

        lax.fori_loop(0, 2, body, 0)

    loads[0].wait()
    reorder(in_r, my_r, 1)
    loads[1].wait()
    reorder(in_p, my_p, 3)
    for side in (0, 1):
        for a, b in ((my_r, pk_r), (my_p, pk_p)):
            for r in range(5):
                b[side, r] = a[:, r + 27 * side, :]

    def by_core(action):
        for c in (0, 1):
            pl.when(core == c)(functools.partial(action, c))

    def pack_corners(c):
        part = slice(12, 16) if c == 1 else slice(0, 4)
        for group, row in enumerate((0, 28, 12, 16)):
            for k, a in enumerate((my_r, my_p)):
                for r in range(4):
                    for z in range(4):
                        pk_c[group, k, r, 4 * z : 4 * z + 4, :] = a[part, row + r, lanes(z)]

    by_core(pack_corners)
    blocks[0].start()
    blocks[1].start()
    pl.semaphore_wait(barrier, count)
    for ok, copy in sends:
        guarded(ok, copy.start)
    loads[2].wait()
    reorder(in_s, my_s, 3)
    for side in (0, 1):
        pk_s[side] = my_s[:, 31 * side, :]
    loads[3].wait()
    reorder(in_b, my_b, 3)
    blocks[2].start()
    blocks[3].start()
    for ok, copy in sends_late:
        guarded(ok, copy.start)

    @pl.when(jnp.logical_not(low))
    def _():
        st_r[0:LO] = jnp.full((LO, 24, 512), float(ROCKS), f32)
        st_p[0:LO] = jnp.zeros((LO, 24, 512), f32)

    @pl.when(jnp.logical_not(high))
    def _():
        st_r[LO + NL :] = jnp.full((5, 24, 512), float(ROCKS), f32)
        st_p[LO + NL :] = jnp.zeros((5, 24, 512), f32)

    @pl.when(jnp.logical_not(outer))
    def _():
        ys_r[...] = jnp.full((5, NL, 512), float(ROCKS), f32)
        ys_p[...] = jnp.zeros((5, NL, 512), f32)
        ys_s[...] = jnp.zeros((NL, 512), f32)

    for side, ok in ((0, low), (1, high)):

        @pl.when(jnp.logical_not(ok & outer))
        def _(side=side):
            co[0, side, 0] = jnp.full((4, 16, 128), float(ROCKS), f32)
            co[0, side, 1] = jnp.zeros((4, 16, 128), f32)

        @pl.when(jnp.logical_not(ok))
        def _(side=side):
            co[1, side, 0] = jnp.full((4, 16, 128), float(ROCKS), f32)
            co[1, side, 1] = jnp.zeros((4, 16, 128), f32)

    well_x, well_y, well_z = wells[0:1, :], wells[1:2, :], wells[2:3, :]
    rate = well_rates[...]
    x0, y0 = NL * xc - LO, NL * gy + LX * core - 4
    columns = depth_of(lax.broadcasted_iota(jnp.int32, (512, WELLS), 0))
    one_z = jnp.where(columns == well_z, 1.0, 0.0).astype(jnp.bfloat16)
    hot_b[:, 0:WELLS] = one_z
    hot_b[:, WELLS:] = one_z
    pair_ids = lax.broadcasted_iota(jnp.int32, (48, WELLS), 0)
    second = pair_ids >= 24
    row_ids = jnp.where(second, pair_ids - 24, pair_ids) + y0
    layer_ids = jnp.where(second, 1, 0) + x0
    high_part = rate.astype(jnp.bfloat16).astype(f32)
    low_part = rate - high_part

    def hot_rows(l, _):
        here = (row_ids == well_y) & (layer_ids == well_x - 2 * l)
        at = pl.ds(pl.multiple_of(48 * l, 16), 48)
        hot_a[at, 0:WELLS] = jnp.where(here, high_part, 0.0).astype(jnp.bfloat16)
        hot_a[at, WELLS:] = jnp.where(here, low_part, 0.0).astype(jnp.bfloat16)
        return 0

    lax.fori_loop(0, (EL + 1) // 2, hot_rows, 0)

    def spread(m, _):
        at = pl.ds(pl.multiple_of(336 * m, 16), 336)
        got = lax.dot_general(
            hot_a[at, :], hot_b[...], (((1,), (1,)), ((), ())), preferred_element_type=f32
        )
        for z in range(4):
            rt[z, pl.ds(14 * m, 14)] = got[:, lanes(z)].reshape(14, 24, 128)
        return 0

    lax.fori_loop(0, 3, spread, 0)

    def table(ref, rule):
        return [rule(jnp.full((8, 128), ref[k], f32)) for k in range(ROCKS)]

    tab_h = table(perm_tab, lambda v: 0.5 / v) + [jnp.full((8, 128), FAR, f32)]
    tab_s = table(poro_tab, lambda v: (COMPRESS * VOLUME) * v) + [jnp.full((8, 128), 1.0, f32)]

    def lookup(kinds, n=8):
        h, s = tab_h[0][:n], tab_s[0][:n]
        for k in range(1, ROCKS + 1):
            later = kinds > k - 0.5
            h = jnp.where(later, tab_h[k][:n], h)
            s = jnp.where(later, tab_s[k][:n], s)
        return h, s

    def unpack_layers(first, last, at_row, tiles=(0, 1, 2)):
        def body(l, _):
            for z in range(4):
                for t in tiles:
                    h, s = lookup(st_r[l, 8 * t : 8 * t + 8, lanes(z)])
                    e = at_row + 8 * t
                    hh[z, l, e : e + 8, :] = h
                    st[z, l, e : e + 8, :] = s
                    pa[z, l, e : e + 8, :] = st_p[l, 8 * t : 8 * t + 8, lanes(z)]
            return 0

        lax.fori_loop(first, last, body, 0)

    for copy in blocks:
        copy.wait()
    arrived(0, st_r.at[pl.ds(LO, LX)])
    arrived(1, st_p.at[pl.ds(LO, LX)])
    by_core(lambda c: unpack_layers(LO, LO + NL, RO - 8 * c))

    def fraction(s):
        q = s * s
        return q * recip(1.5 * q + (0.5 - s))

    arrived(2, st_s.at[pl.ds(0, LX)])
    arrived(3, st_b.at[pl.ds(0, LX)])

    def unpack_fraction(c):
        def body(l, _):
            for z in range(4):
                for t in range(3):
                    e = 8 - 8 * c + 8 * t
                    fs[z, l, e : e + 8, :] = fraction(st_s[l, 8 * t : 8 * t + 8, lanes(z)])
            return 0

        lax.fori_loop(0, NL, body, 0)

    by_core(unpack_fraction)

    arrived(4, ys_r, outer)
    arrived(5, ys_p, outer)
    arrived(6, ys_s, outer)
    rows_here = pl.ds(pl.multiple_of(8 * core, 8), 16)
    arrived(7, st_r.at[pl.ds(0, 4), rows_here, :], low)
    arrived(8, st_p.at[pl.ds(0, 4), rows_here, :], low)
    arrived(9, st_r.at[pl.ds(LO + NL, 5), rows_here, :], high)
    arrived(10, st_p.at[pl.ds(LO + NL, 5), rows_here, :], high)
    arrived(11, co.at[0, 0], low & outer)
    arrived(12, co.at[0, 1], high & outer)
    arrived(13, co.at[1, 0], low)
    arrived(14, co.at[1, 1], high)

    def unpack_halo(c):
        unpack_layers(0, LO, RO - 8 * c, (c, c + 1))
        unpack_layers(LO + NL, EL, RO - 8 * c, (c, c + 1))
        e = 7 if c == 0 else 28

        for z in range(4):
            for r in range(5):
                for g in range(4):
                    at = pl.ds(LO + 8 * g, 8)
                    h, s = lookup(ys_r[r, 8 * g : 8 * g + 8, lanes(z)])
                    hh[z, at, e + r, :] = h
                    st[z, at, e + r, :] = s
                    pa[z, at, e + r, :] = ys_p[r, 8 * g : 8 * g + 8, lanes(z)]
            for kind in (0, 1):
                e4 = 8 if c == kind else 28
                for r in range(4):
                    for side, place in ((0, 0), (1, LO + NL)):
                        at = pl.ds(place, 4)
                        h, s = lookup(co[kind, side, 0, r, 4 * z : 4 * z + 4, :], 4)
                        hh[z, at, e4 + r, :] = h
                        st[z, at, e4 + r, :] = s
                        pa[z, at, e4 + r, :] = co[kind, side, 1, r, 4 * z : 4 * z + 4, :]
            fs[z, :, 7 if c == 0 else 24, :] = fraction(ys_s[:, lanes(z)])

    by_core(unpack_halo)

    lane = lax.broadcasted_iota(jnp.int32, (24, 128), 1)
    last = lane == 127

    def side_faces(l):
        for z in range(4):
            te[z, l, 8:32, :] = recip(hh[z, l, 8:32, :] + hh[z, l + 1, 8:32, :])
            tn[z, l, 0:32, :] = recip(hh[z, l, 0:32, :] + hh[z, l, 1:33, :])

    layers(0, EL - 1, 2, side_faces)

    def weights(l):
        own_h = [hh[z, l, 8:32, :] for z in range(4)]
        deeper = next_z(own_h)
        below = [recip(own_h[z] + deeper[z]) for z in range(4)]
        below[3] = jnp.where(last, 0.0, below[3])
        above = prev_z(below)
        for z in (1, 2, 3, 0):
            tb[z, l, 8:32, :] = below[z]
            storage = st[z, l, 8:32, :]
            diagonal = (
                storage + te[z, l, 8:32, :] + te[z, l - 1, 8:32, :]
                + tn[z, l, 8:32, :] + tn[z, l, 7:31, :] + below[z] + above[z]
            )
            ww[z, l, 8:32, :] = OMEGA * recip(diagonal)
            src[z, l, 8:32, :] = storage * pa[z, l, 8:32, :] + rt[z, l]

    layers(1, EL - 1, 3, weights)

    def one_pass(old, new, start, stop):
        def body(l):
            here = [old[z, l, 8:32, :] for z in range(4)]
            faces = [tb[z, l, 8:32, :] for z in range(4)]
            deeper = next_z(here)
            shallower = prev_z([faces[z] * here[z] for z in range(4)])
            for z in (1, 2, 3, 0):
                total = (
                    src[z, l, 8:32, :] + faces[z] * deeper[z] + shallower[z]
                    + te[z, l, 8:32, :] * old[z, l + 1, 8:32, :]
                    + te[z, l - 1, 8:32, :] * old[z, l - 1, 8:32, :]
                    + tn[z, l, 8:32, :] * old[z, l, 9:33, :]
                    + tn[z, l, 7:31, :] * old[z, l, 7:31, :]
                )
                new[z, l, 8:32, :] = (1.0 - OMEGA) * here[z] + ww[z, l, 8:32, :] * total

        layers(start, stop, 3, body)

    one_pass(pa, pb, 1, 40)
    one_pass(pb, pa, 2, 39)
    one_pass(pa, pb, 3, 38)
    one_pass(pb, pa, 4, 37)

    def fluxes(l):
        e = l + LO
        center = [pa[z, e, RO : RO + 16, :] for z in range(4)]
        frac = [fs[z, l, 8:24, :] for z in range(4)]
        deeper, frac_deep = next_z(center), next_z(frac)
        drained = []
        for z in range(4):
            flow = tb[z, e, RO : RO + 16, :] * (center[z] - deeper[z])
            drained.append(flow * jnp.where(flow > 0, frac[z], frac_deep[z]))
        entered = prev_z(drained)
        at = pl.ds(pl.multiple_of(8 * core, 8), 16)
        for z in range(4):
            p, f = center[z], frac[z]
            res_p[l, :, lanes(z)] = p
            through = jnp.maximum(
                st_b[l, :, lanes(z)] + te[z, e, RO : RO + 16, :] * (p - pa[z, e + 1, RO : RO + 16, :]), 0.0
            )
            north = tn[z, e, RO : RO + 16, :] * (p - pa[z, e, RO + 1 : RO + 17, :])
            south = tn[z, e, RO - 1 : RO + 15, :] * (p - pa[z, e, RO - 1 : RO + 15, :])
            leaving = drained[z] - entered[z]
            leaving = leaving + north * jnp.where(north > 0, f, fs[z, l, 9:25, :])
            leaving = leaving + south * jnp.where(south > 0, f, fs[z, l, 7:23, :])
            rates = rt[z, e, 4:20, :]
            extra = rates * jnp.where(rates > 0, 1.0, f) - leaving
            per_volume = recip((1.0 / COMPRESS) * st[z, e, RO : RO + 16, :])
            s = st_s[l, at, lanes(z)]
            q = s * s
            inverse = recip(1.5 * q + (0.5 - s))
            slope = (s - q) * inverse * inverse
            extra = extra * per_volume
            relative = through * per_volume
            step = recip(1.0 + relative * slope)
            hh[z, l, 8:24, :] = s + extra
            hh[z, l, 24:40, :] = per_volume
            pb[z, l, 8:24, :] = s + (extra - relative * f) * step
            pb[z, l, 24:40, :] = per_volume * step
            ww[z, l, 8:24, :] = relative
            ww[z, l, 24:40, :] = through

    layers(0, NL, 2, fluxes)

    theirs = pl.ds(LX * (1 - core), LX)
    out_rows = pl.ds(pl.multiple_of(16 * core, 16), 16)
    keep_p = local(8, res_p.at[own0], out_p.at[:, out_rows, :])
    give_p = remote(18, 15, res_p.at[theirs], out_p.at[:, out_rows, :], partner)

    def restore(ref, first, count):
        at = pl.ds(first, count)
        value = ref[at].reshape(16 * count, 512)
        ref[at] = permuted(value, back[...], 3).reshape(count, 16, 512)

    def hand_back_pressure():
        for first in (0, 16):
            restore(res_p, first, 16)
        keep_p.start()
        give_p.start()

    pl.when(low)(hand_back_pressure)

    def newton(s, c, relative):
        q = s * s
        d = 1.5 * q + (0.5 - s)
        return d * d + relative * (s - q), d * (d * (s - c) + relative * q)

    waves, keeps, gives = [], [], []
    for half in (0, 1):
        tiles = (2 * half, 2 * half + 1)
        wide = pl.ds(256 * half, 256)
        waves.append(remote(19 + half, 16 + half, face_out.at[half], face_in.at[half], (gx + 2, gy)))
        keeps.append(local(10 + half, res_s.at[own0, :, wide], out_s.at[:, out_rows, wide]))
        gives.append(remote(21 + half, 18 + half, res_s.at[theirs, :, wide], out_s.at[:, out_rows, wide], partner))

        @pl.when(jnp.logical_not(low))
        def _(half=half, tiles=tiles):
            for z in tiles:
                face_in[half, z % 2] = st_b[0, :, lanes(z)]

        arrived(16 + half, face_in.at[half], low)

        def sweep(l, coming, tiles=tiles):
            going = []
            for z in tiles:
                relative = ww[z, l, 8:24, :]
                inflow = coming[z % 2]
                c = hh[z, l, 8:24, :] + hh[z, l, 24:40, :] * inflow
                s = jnp.clip(pb[z, l, 8:24, :] + pb[z, l, 24:40, :] * inflow, 0.0, 1.0)
                below, above = newton(s, c, relative)
                s = jnp.clip(s - above * recip(below), 0.0, 1.0)
                below, above = newton(s, c, relative)
                top = jnp.minimum(jnp.maximum(s * below - above, 0.0), below)
                res_s[l, :, lanes(z)] = top * recip(below)
                rest = (below - top) * (MOBILITY**0.5)
                top = top * top
                going.append(ww[z, l, 24:40, :] * top * recip(top + rest * rest))
            return going

        coming = lax.fori_loop(0, NL, sweep, [face_in[half, 0], face_in[half, 1]])
        for z in (0, 1):
            face_out[half, z] = coming[z]
        pl.when(high)(waves[half].start)
        keeps[half].start()
        gives[half].start()

    pl.when(jnp.logical_not(low))(hand_back_pressure)

    for ok, copy in sends + sends_late:
        guarded(ok, copy.wait_send)
    keep_p.wait()
    give_p.wait()
    for half in (0, 1):
        keeps[half].wait()
        pl.when(high)(waves[half].wait_send)
        gives[half].wait()


def finish_kernel(p_in, s_in, p_out, s_out, held, back, sem):
    across = pltpu.make_async_copy(p_in, p_out, sem.at[0])
    across.start()
    parts = []
    for i in range(4):
        at = pl.ds(4 * i, 4)
        parts.append((
            pltpu.make_async_copy(s_in.at[at], held.at[at], sem.at[1 + i]),
            pltpu.make_async_copy(held.at[at], s_out.at[at], sem.at[5 + i]),
        ))
        parts[i][0].start()
    ahead = lax.broadcasted_iota(jnp.int32, (512, 512), 0)
    aside = lax.broadcasted_iota(jnp.int32, (512, 512), 1)
    back[...] = jnp.where(4 * lax.rem(ahead, 128) + ahead // 128 == aside, 1.0, 0.0).astype(jnp.bfloat16)
    for i in range(4):
        parts[i][0].wait()
        at = pl.ds(4 * i, 4)
        value = held[at].reshape(128, 512)
        held[at] = permuted(value, back[...], 3).reshape(4, 32, 512)
        parts[i][1].start()
    for i in range(4):
        parts[i][1].wait()
    across.wait()


def shards(rock, perm_tab, poro_tab, base, press, sat0, wells, well_rates):
    f32, i32 = jnp.float32, jnp.int32
    shape = jax.ShapeDtypeStruct(rock.shape, f32)
    hbm = pl.BlockSpec(memory_space=pl.ANY)
    smem = pl.BlockSpec(memory_space=pltpu.SMEM)
    vmem = pl.BlockSpec(memory_space=pltpu.VMEM)
    extended = pltpu.VMEM((4, EL, ER, 128), f32)
    block = pltpu.VMEM((LX, 32, 512), f32)
    halfway = pl.pallas_call(
        step_kernel,
        out_shape=(shape, shape),
        in_specs=[hbm, smem, smem, hbm, hbm, hbm, vmem, vmem],
        out_specs=(hbm, hbm),
        scratch_shapes=[
            pltpu.VMEM((EL, 24, 512), f32),
            pltpu.VMEM((EL, 24, 512), f32),
            pltpu.VMEM((NL, 24, 512), f32),
            pltpu.VMEM((NL, 16, 512), f32),
            pltpu.VMEM((LX, 32, 512), i32),
            block, block, block, block, block, block, block,
            pltpu.VMEM((2, 5, LX, 512), f32),
            pltpu.VMEM((2, 5, LX, 512), f32),
            pltpu.VMEM((2, LX, 512), f32),
            pltpu.VMEM((4, 2, 4, 16, 128), f32),
            pltpu.VMEM((5, NL, 512), f32),
            pltpu.VMEM((5, NL, 512), f32),
            pltpu.VMEM((NL, 512), f32),
            pltpu.VMEM((2, 2, 2, 4, 16, 128), f32),
            extended, extended, extended, extended, extended, extended, extended, extended, extended,
            pltpu.VMEM((4, EL + 1, 24, 128), f32),
            pltpu.VMEM((24 * (EL + 1), 2 * WELLS), jnp.bfloat16),
            pltpu.VMEM((512, 2 * WELLS), jnp.bfloat16),
            pltpu.VMEM((4, NL, 32, 128), f32),
            pltpu.VMEM((512, 512), jnp.bfloat16),
            pltpu.VMEM((512, 512), jnp.bfloat16),
            pltpu.VMEM((2, 2, 16, 128), f32),
            pltpu.VMEM((2, 2, 16, 128), f32),
            pltpu.VMEM((NL, 16, 512), f32),
            pltpu.VMEM((NL, 16, 512), f32),
            pltpu.SemaphoreType.DMA((12,)),
            pltpu.SemaphoreType.DMA((23,)),
            pltpu.SemaphoreType.DMA((20,)),
        ],
        compiler_params=pltpu.CompilerParams(
            collective_id=0, has_side_effects=True, vmem_limit_bytes=60 * 1024 * 1024
        ),
    )(rock, perm_tab, poro_tab, base, press, sat0, wells, well_rates.reshape(1, WELLS))
    return pl.pallas_call(
        finish_kernel,
        out_shape=(shape, shape),
        in_specs=[hbm, hbm],
        out_specs=(hbm, hbm),
        scratch_shapes=[block, pltpu.VMEM((512, 512), jnp.bfloat16), pltpu.SemaphoreType.DMA((9,))],
        compiler_params=pltpu.CompilerParams(vmem_limit_bytes=60 * 1024 * 1024),
    )(*halfway)


def solution(mesh):
    block = P("gx", "gy", None)
    return jax.shard_map(
        shards,
        mesh=mesh,
        in_specs=(block, P(), P(), block, block, block, P(), P()),
        out_specs=(block, block),
        check_vma=False,
    )
```

```python
import functools

import jax
import jax.numpy as jnp
from jax import lax
from jax.experimental import pallas as pl
from jax.experimental.pallas import tpu as pltpu
from jax.sharding import PartitionSpec as P

PASSES = 4
MOBILITY = 0.5
OMEGA = 0.8
VOLUME = 4.0
COMPRESS = 0.5

MESH = pl.DeviceIdType.MESH
LX = 16
NL = 32
EL = 41
LO = 4
ER = 40
RO = 12
ROCKS = 8
FAR = 1e30
NXC = 4
NGY = 16
WELLS = 512


def roll(value, shift):
    return pltpu.roll(value, shift % 128, 1)


def next_z(tiles):
    return [tiles[1], tiles[2], tiles[3], roll(tiles[0], -1)]


def prev_z(tiles):
    return [roll(tiles[3], 1), tiles[0], tiles[1], tiles[2]]


def layers(start, stop, block, body):
    whole = (stop - start) // block

    def several(i, _):
        for j in range(block):
            body(start + block * i + j)
        return 0

    lax.fori_loop(0, whole, several, 0)
    for l in range(start + block * whole, stop):
        body(l)


def recip(value):
    return pl.reciprocal(value, approx=False)


def permuted(value, matrix, parts):
    total, rest = None, value
    for k in range(parts):
        piece = rest.astype(jnp.bfloat16)
        term = jnp.dot(piece, matrix, preferred_element_type=jnp.float32)
        total = term if total is None else total + term
        if k < parts - 1:
            rest = rest - piece.astype(jnp.float32)
    return total


def lanes(z):
    return slice(128 * z, 128 * z + 128)


def step_kernel(
    rock, perm_tab, poro_tab, base, press, sat0, wells, well_rates,
    out_p, out_s,
    st_r, st_p, st_s, st_b,
    in_r, in_p, in_s, in_b, my_r, my_p, my_s, my_b, pk_r, pk_p, pk_s, pk_c, ys_r, ys_p, ys_s, co,
    hh, st, pa, pb, te, tn, tb, ww, src, rt, hot_a, hot_b, fs, order, back,
    face_in, face_out, res_p, res_s,
    loc, snd, rcv,
):
    gx, gy = lax.axis_index("gx"), lax.axis_index("gy")
    xc, core = gx // 2, lax.rem(gx, 2)
    partner = (gx + 1 - 2 * core, gy)
    low, high = xc > 0, xc < NXC - 1
    down, up = gy > 0, gy < NGY - 1
    f32 = jnp.float32

    barrier = pltpu.get_barrier_semaphore()
    count = jnp.int32(0)
    for dx in (-1, 0, 1):
        for dy in (-1, 0, 1):
            for other in (0, 1):
                there = (xc + dx >= 0) & (xc + dx < NXC) & (gy + dy >= 0) & (gy + dy < NGY)
                if dx == 0 and dy == 0:
                    there = there & (core != other)
                count = count + there.astype(jnp.int32)

                @pl.when(there)
                def _(dx=dx, dy=dy, other=other):
                    pl.semaphore_signal(
                        barrier, inc=1, device_id=(2 * (xc + dx) + other, gy + dy), device_id_type=MESH
                    )

    def local(k, a, b):
        return pltpu.make_async_copy(a, b, loc.at[k])

    row24 = pl.ds(pl.multiple_of(8 * core, 8), 24)
    row16 = pl.ds(pl.multiple_of(16 * core, 16), 16)
    own = pl.ds(LO + LX * core, LX)
    own0 = pl.ds(LX * core, LX)
    loads = [
        local(0, rock, in_r), local(1, press, in_p), local(2, sat0, in_s), local(3, base, in_b)
    ]
    for copy in loads:
        copy.start()
    blocks = [
        local(4, my_r.at[:, row24, :], st_r.at[own]),
        local(5, my_p.at[:, row24, :], st_p.at[own]),
        local(6, my_s.at[:, row24, :], st_s.at[own0]),
        local(7, my_b.at[:, row16, :], st_b.at[own0]),
    ]

    def remote(k, j, a, b, device):
        return pltpu.make_async_remote_copy(
            src_ref=a, dst_ref=b, send_sem=snd.at[k], recv_sem=rcv.at[j], device_id=device, device_id_type=MESH
        )

    other24 = pl.ds(pl.multiple_of(8 * (1 - core), 8), 24)
    other16 = pl.ds(pl.multiple_of(16 * (1 - core), 16), 16)
    sends = []
    ypart = pl.ds(pl.multiple_of(LX * core, 16), LX)
    last_layers, first_layers = (core == 1) & high, (core == 0) & low
    for k, (a, b, pk, ys) in enumerate(((my_r, st_r, pk_r, ys_r), (my_p, st_p, pk_p, ys_p))):
        for side, ok, device in ((0, down, (2 * xc + 1, gy - 1)), (1, up, (2 * xc, gy + 1))):
            sends.append((ok, remote(4 + 2 * k + side, 4 + k, pk.at[side], ys.at[:, ypart, :], device)))
        for d in (0, 1):
            rows, place = pl.ds(16 * d, 16), pl.ds(8 * d, 16)
            sends.append((last_layers, remote(
                8 + 2 * d + k, 7 + k, a.at[pl.ds(12, 4), rows, :], b.at[pl.ds(0, 4), place, :], (2 * (xc + 1) + d, gy),
            )))
            sends.append((first_layers, remote(
                8 + 2 * d + k, 9 + k, a.at[pl.ds(0, 5), rows, :], b.at[pl.ds(LO + NL, 5), place, :], (2 * (xc - 1) + d, gy),
            )))
        sends.append((None, remote(k, k, a.at[:, other24, :], b.at[own], partner)))
    for group, (ok, d, dy, kind) in enumerate(((down, 1, -1, 0), (up, 0, 1, 0), (None, 1, 0, 1), (None, 0, 0, 1))):
        for part, side, dx in ((last_layers, 0, 1), (first_layers, 1, -1)):
            sends.append((
                part if ok is None else part & ok,
                remote(12 + group, 11 + 2 * kind + side, pk_c.at[group], co.at[kind, side], (2 * (xc + dx) + d, gy + dy)),
            ))
    sends_late = []
    for side, ok, device in ((0, down, (2 * xc + 1, gy - 1)), (1, up, (2 * xc, gy + 1))):
        sends_late.append((ok, remote(16 + side, 6, pk_s.at[side], ys_s.at[ypart, :], device)))
    sends_late.append((None, remote(2, 2, my_s.at[:, other24, :], st_s.at[own0], partner)))
    sends_late.append((None, remote(3, 3, my_b.at[:, other16, :], st_b.at[own0], partner)))

    def guarded(ok, action):
        if ok is None:
            action()
        else:
            pl.when(ok)(action)

    def arrived(k, ref, ok=None):
        guarded(ok, lambda: pltpu.make_async_copy(ref, ref, rcv.at[k]).wait())

    outer = ((core == 0) & down) | ((core == 1) & up)

    def depth_of(place):
        return 4 * lax.rem(place, 128) + place // 128

    ahead = lax.broadcasted_iota(jnp.int32, (512, 512), 0)
    aside = lax.broadcasted_iota(jnp.int32, (512, 512), 1)
    order[...] = jnp.where(ahead == depth_of(aside), 1.0, 0.0).astype(jnp.bfloat16)
    back[...] = jnp.where(depth_of(ahead) == aside, 1.0, 0.0).astype(jnp.bfloat16)

    def reorder(a, b, parts):
        def body(m, _):
            at = pl.ds(pl.multiple_of(8 * m, 8), 8)
            value = a[at].reshape(256, 512).astype(f32)
            b[at] = permuted(value, order[...], parts).reshape(8, 32, 512)
            return 0

        lax.fori_loop(0, 2, body, 0)

    loads[0].wait()
    reorder(in_r, my_r, 1)
    loads[1].wait()
    reorder(in_p, my_p, 3)
    for side in (0, 1):
        for a, b in ((my_r, pk_r), (my_p, pk_p)):
            for r in range(5):
                b[side, r] = a[:, r + 27 * side, :]

    def by_core(action):
        for c in (0, 1):
            pl.when(core == c)(functools.partial(action, c))

    def pack_corners(c):
        part = slice(12, 16) if c == 1 else slice(0, 4)
        for group, row in enumerate((0, 28, 12, 16)):
            for k, a in enumerate((my_r, my_p)):
                for r in range(4):
                    for z in range(4):
                        pk_c[group, k, r, 4 * z : 4 * z + 4, :] = a[part, row + r, lanes(z)]

    by_core(pack_corners)
    blocks[0].start()
    blocks[1].start()
    pl.semaphore_wait(barrier, count)
    for ok, copy in sends:
        guarded(ok, copy.start)
    loads[2].wait()
    reorder(in_s, my_s, 3)
    for side in (0, 1):
        pk_s[side] = my_s[:, 31 * side, :]
    loads[3].wait()
    reorder(in_b, my_b, 3)
    blocks[2].start()
    blocks[3].start()
    for ok, copy in sends_late:
        guarded(ok, copy.start)

    @pl.when(jnp.logical_not(low))
    def _():
        st_r[0:LO] = jnp.full((LO, 24, 512), float(ROCKS), f32)
        st_p[0:LO] = jnp.zeros((LO, 24, 512), f32)

    @pl.when(jnp.logical_not(high))
    def _():
        st_r[LO + NL :] = jnp.full((5, 24, 512), float(ROCKS), f32)
        st_p[LO + NL :] = jnp.zeros((5, 24, 512), f32)

    @pl.when(jnp.logical_not(outer))
    def _():
        ys_r[...] = jnp.full((5, NL, 512), float(ROCKS), f32)
        ys_p[...] = jnp.zeros((5, NL, 512), f32)
        ys_s[...] = jnp.zeros((NL, 512), f32)

    for side, ok in ((0, low), (1, high)):

        @pl.when(jnp.logical_not(ok & outer))
        def _(side=side):
            co[0, side, 0] = jnp.full((4, 16, 128), float(ROCKS), f32)
            co[0, side, 1] = jnp.zeros((4, 16, 128), f32)

        @pl.when(jnp.logical_not(ok))
        def _(side=side):
            co[1, side, 0] = jnp.full((4, 16, 128), float(ROCKS), f32)
            co[1, side, 1] = jnp.zeros((4, 16, 128), f32)

    well_x, well_y, well_z = wells[0:1, :], wells[1:2, :], wells[2:3, :]
    rate = well_rates[...]
    x0, y0 = NL * xc - LO, NL * gy + LX * core - 4
    columns = depth_of(lax.broadcasted_iota(jnp.int32, (512, WELLS), 0))
    one_z = jnp.where(columns == well_z, 1.0, 0.0).astype(jnp.bfloat16)
    hot_b[:, 0:WELLS] = one_z
    hot_b[:, WELLS:] = one_z
    pair_ids = lax.broadcasted_iota(jnp.int32, (48, WELLS), 0)
    second = pair_ids >= 24
    row_ids = jnp.where(second, pair_ids - 24, pair_ids) + y0
    layer_ids = jnp.where(second, 1, 0) + x0
    high_part = rate.astype(jnp.bfloat16).astype(f32)
    low_part = rate - high_part

    def hot_rows(l, _):
        here = (row_ids == well_y) & (layer_ids == well_x - 2 * l)
        at = pl.ds(pl.multiple_of(48 * l, 16), 48)
        hot_a[at, 0:WELLS] = jnp.where(here, high_part, 0.0).astype(jnp.bfloat16)
        hot_a[at, WELLS:] = jnp.where(here, low_part, 0.0).astype(jnp.bfloat16)
        return 0

    lax.fori_loop(0, (EL + 1) // 2, hot_rows, 0)

    def spread(m, _):
        at = pl.ds(pl.multiple_of(336 * m, 16), 336)
        got = lax.dot_general(
            hot_a[at, :], hot_b[...], (((1,), (1,)), ((), ())), preferred_element_type=f32
        )
        for z in range(4):
            rt[z, pl.ds(14 * m, 14)] = got[:, lanes(z)].reshape(14, 24, 128)
        return 0

    lax.fori_loop(0, 3, spread, 0)

    def table(ref, rule):
        return [rule(jnp.full((8, 128), ref[k], f32)) for k in range(ROCKS)]

    tab_h = table(perm_tab, lambda v: 0.5 / v) + [jnp.full((8, 128), FAR, f32)]
    tab_s = table(poro_tab, lambda v: (COMPRESS * VOLUME) * v) + [jnp.full((8, 128), 1.0, f32)]

    def lookup(kinds, n=8):
        h, s = tab_h[0][:n], tab_s[0][:n]
        for k in range(1, ROCKS + 1):
            later = kinds > k - 0.5
            h = jnp.where(later, tab_h[k][:n], h)
            s = jnp.where(later, tab_s[k][:n], s)
        return h, s

    def unpack_layers(first, last, at_row, tiles=(0, 1, 2)):
        def body(l, _):
            for z in range(4):
                for t in tiles:
                    h, s = lookup(st_r[l, 8 * t : 8 * t + 8, lanes(z)])
                    e = at_row + 8 * t
                    hh[z, l, e : e + 8, :] = h
                    st[z, l, e : e + 8, :] = s
                    pa[z, l, e : e + 8, :] = st_p[l, 8 * t : 8 * t + 8, lanes(z)]
            return 0

        lax.fori_loop(first, last, body, 0)

    for copy in blocks:
        copy.wait()
    arrived(0, st_r.at[pl.ds(LO, LX)])
    arrived(1, st_p.at[pl.ds(LO, LX)])
    by_core(lambda c: unpack_layers(LO, LO + NL, RO - 8 * c))

    def fraction(s):
        q = s * s
        return q * recip(1.5 * q + (0.5 - s))

    arrived(2, st_s.at[pl.ds(0, LX)])
    arrived(3, st_b.at[pl.ds(0, LX)])

    def unpack_fraction(c):
        def body(l, _):
            for z in range(4):
                for t in range(3):
                    e = 8 - 8 * c + 8 * t
                    fs[z, l, e : e + 8, :] = fraction(st_s[l, 8 * t : 8 * t + 8, lanes(z)])
            return 0

        lax.fori_loop(0, NL, body, 0)

    by_core(unpack_fraction)

    arrived(4, ys_r, outer)
    arrived(5, ys_p, outer)
    arrived(6, ys_s, outer)
    rows_here = pl.ds(pl.multiple_of(8 * core, 8), 16)
    arrived(7, st_r.at[pl.ds(0, 4), rows_here, :], low)
    arrived(8, st_p.at[pl.ds(0, 4), rows_here, :], low)
    arrived(9, st_r.at[pl.ds(LO + NL, 5), rows_here, :], high)
    arrived(10, st_p.at[pl.ds(LO + NL, 5), rows_here, :], high)
    arrived(11, co.at[0, 0], low & outer)
    arrived(12, co.at[0, 1], high & outer)
    arrived(13, co.at[1, 0], low)
    arrived(14, co.at[1, 1], high)

    def unpack_halo(c):
        unpack_layers(0, LO, RO - 8 * c, (c, c + 1))
        unpack_layers(LO + NL, EL, RO - 8 * c, (c, c + 1))
        e = 7 if c == 0 else 28

        for z in range(4):
            for r in range(5):
                for g in range(4):
                    at = pl.ds(LO + 8 * g, 8)
                    h, s = lookup(ys_r[r, 8 * g : 8 * g + 8, lanes(z)])
                    hh[z, at, e + r, :] = h
                    st[z, at, e + r, :] = s
                    pa[z, at, e + r, :] = ys_p[r, 8 * g : 8 * g + 8, lanes(z)]
            for kind in (0, 1):
                e4 = 8 if c == kind else 28
                for r in range(4):
                    for side, place in ((0, 0), (1, LO + NL)):
                        at = pl.ds(place, 4)
                        h, s = lookup(co[kind, side, 0, r, 4 * z : 4 * z + 4, :], 4)
                        hh[z, at, e4 + r, :] = h
                        st[z, at, e4 + r, :] = s
                        pa[z, at, e4 + r, :] = co[kind, side, 1, r, 4 * z : 4 * z + 4, :]
            fs[z, :, 7 if c == 0 else 24, :] = fraction(ys_s[:, lanes(z)])

    by_core(unpack_halo)

    lane = lax.broadcasted_iota(jnp.int32, (24, 128), 1)
    last = lane == 127

    def side_faces(l):
        for z in range(4):
            te[z, l, 8:32, :] = recip(hh[z, l, 8:32, :] + hh[z, l + 1, 8:32, :])
            tn[z, l, 0:32, :] = recip(hh[z, l, 0:32, :] + hh[z, l, 1:33, :])

    layers(0, EL - 1, 2, side_faces)

    def weights(l):
        own_h = [hh[z, l, 8:32, :] for z in range(4)]
        deeper = next_z(own_h)
        below = [recip(own_h[z] + deeper[z]) for z in range(4)]
        below[3] = jnp.where(last, 0.0, below[3])
        above = prev_z(below)
        for z in (1, 2, 3, 0):
            tb[z, l, 8:32, :] = below[z]
            storage = st[z, l, 8:32, :]
            diagonal = (
                storage + te[z, l, 8:32, :] + te[z, l - 1, 8:32, :]
                + tn[z, l, 8:32, :] + tn[z, l, 7:31, :] + below[z] + above[z]
            )
            ww[z, l, 8:32, :] = OMEGA * recip(diagonal)
            src[z, l, 8:32, :] = storage * pa[z, l, 8:32, :] + rt[z, l]

    layers(1, EL - 1, 3, weights)

    def one_pass(old, new, start, stop):
        def body(l):
            here = [old[z, l, 8:32, :] for z in range(4)]
            faces = [tb[z, l, 8:32, :] for z in range(4)]
            deeper = next_z(here)
            shallower = prev_z([faces[z] * here[z] for z in range(4)])
            for z in (1, 2, 3, 0):
                total = (
                    src[z, l, 8:32, :] + faces[z] * deeper[z] + shallower[z]
                    + te[z, l, 8:32, :] * old[z, l + 1, 8:32, :]
                    + te[z, l - 1, 8:32, :] * old[z, l - 1, 8:32, :]
                    + tn[z, l, 8:32, :] * old[z, l, 9:33, :]
                    + tn[z, l, 7:31, :] * old[z, l, 7:31, :]
                )
                new[z, l, 8:32, :] = (1.0 - OMEGA) * here[z] + ww[z, l, 8:32, :] * total

        layers(start, stop, 3, body)

    one_pass(pa, pb, 1, 40)
    one_pass(pb, pa, 2, 39)
    one_pass(pa, pb, 3, 38)
    one_pass(pb, pa, 4, 37)

    def fluxes(l):
        e = l + LO
        center = [pa[z, e, RO : RO + 16, :] for z in range(4)]
        frac = [fs[z, l, 8:24, :] for z in range(4)]
        deeper, frac_deep = next_z(center), next_z(frac)
        drained = []
        for z in range(4):
            flow = tb[z, e, RO : RO + 16, :] * (center[z] - deeper[z])
            drained.append(flow * jnp.where(flow > 0, frac[z], frac_deep[z]))
        entered = prev_z(drained)
        at = pl.ds(pl.multiple_of(8 * core, 8), 16)
        for z in range(4):
            p, f = center[z], frac[z]
            res_p[l, :, lanes(z)] = p
            through = jnp.maximum(
                st_b[l, :, lanes(z)] + te[z, e, RO : RO + 16, :] * (p - pa[z, e + 1, RO : RO + 16, :]), 0.0
            )
            north = tn[z, e, RO : RO + 16, :] * (p - pa[z, e, RO + 1 : RO + 17, :])
            south = tn[z, e, RO - 1 : RO + 15, :] * (p - pa[z, e, RO - 1 : RO + 15, :])
            leaving = drained[z] - entered[z]
            leaving = leaving + north * jnp.where(north > 0, f, fs[z, l, 9:25, :])
            leaving = leaving + south * jnp.where(south > 0, f, fs[z, l, 7:23, :])
            rates = rt[z, e, 4:20, :]
            extra = rates * jnp.where(rates > 0, 1.0, f) - leaving
            per_volume = recip((1.0 / COMPRESS) * st[z, e, RO : RO + 16, :])
            s = st_s[l, at, lanes(z)]
            q = s * s
            inverse = recip(1.5 * q + (0.5 - s))
            slope = (s - q) * inverse * inverse
            extra = extra * per_volume
            relative = through * per_volume
            step = recip(1.0 + relative * slope)
            hh[z, l, 8:24, :] = s + extra
            hh[z, l, 24:40, :] = per_volume
            pb[z, l, 8:24, :] = s + (extra - relative * f) * step
            pb[z, l, 24:40, :] = per_volume * step
            ww[z, l, 8:24, :] = relative
            ww[z, l, 24:40, :] = through

    layers(0, NL, 2, fluxes)

    theirs = pl.ds(LX * (1 - core), LX)
    out_rows = pl.ds(pl.multiple_of(16 * core, 16), 16)
    keep_p = local(8, res_p.at[own0], out_p.at[:, out_rows, :])
    give_p = remote(18, 15, res_p.at[theirs], out_p.at[:, out_rows, :], partner)

    def restore(ref, first, count):
        at = pl.ds(first, count)
        value = ref[at].reshape(16 * count, 512)
        ref[at] = permuted(value, back[...], 3).reshape(count, 16, 512)

    def hand_back_pressure():
        for first in (0, 16):
            restore(res_p, first, 16)
        keep_p.start()
        give_p.start()

    pl.when(low)(hand_back_pressure)

    def newton(s, c, relative):
        q = s * s
        d = 1.5 * q + (0.5 - s)
        return d * d + relative * (s - q), d * (d * (s - c) + relative * q)

    waves, keeps, gives = [], [], []
    for half in (0, 1):
        tiles = (2 * half, 2 * half + 1)
        wide = pl.ds(256 * half, 256)
        waves.append(remote(19 + half, 16 + half, face_out.at[half], face_in.at[half], (gx + 2, gy)))
        keeps.append(local(10 + half, res_s.at[own0, :, wide], out_s.at[:, out_rows, wide]))
        gives.append(remote(21 + half, 18 + half, res_s.at[theirs, :, wide], out_s.at[:, out_rows, wide], partner))

        @pl.when(jnp.logical_not(low))
        def _(half=half, tiles=tiles):
            for z in tiles:
                face_in[half, z % 2] = st_b[0, :, lanes(z)]

        arrived(16 + half, face_in.at[half], low)

        def sweep(l, coming, tiles=tiles):
            going = []
            for z in tiles:
                relative = ww[z, l, 8:24, :]
                inflow = coming[z % 2]
                c = hh[z, l, 8:24, :] + hh[z, l, 24:40, :] * inflow
                s = jnp.clip(pb[z, l, 8:24, :] + pb[z, l, 24:40, :] * inflow, 0.0, 1.0)
                below, above = newton(s, c, relative)
                s = jnp.clip(s - above * recip(below), 0.0, 1.0)
                below, above = newton(s, c, relative)
                top = jnp.minimum(jnp.maximum(s * below - above, 0.0), below)
                res_s[l, :, lanes(z)] = top * recip(below)
                rest = (below - top) * (MOBILITY**0.5)
                top = top * top
                going.append(ww[z, l, 24:40, :] * top * recip(top + rest * rest))
            return going

        coming = lax.fori_loop(0, NL, sweep, [face_in[half, 0], face_in[half, 1]])
        for z in (0, 1):
            face_out[half, z] = coming[z]
        pl.when(high)(waves[half].start)
        keeps[half].start()
        gives[half].start()

    pl.when(jnp.logical_not(low))(hand_back_pressure)

    for ok, copy in sends + sends_late:
        guarded(ok, copy.wait_send)
    keep_p.wait()
    give_p.wait()
    for half in (0, 1):
        keeps[half].wait()
        pl.when(high)(waves[half].wait_send)
        gives[half].wait()


def finish_kernel(p_in, s_in, p_out, s_out, held_p, held, back, sem):
    parts, plain = [], []
    for i in range(4):
        at = pl.ds(4 * i, 4)
        parts.append((
            pltpu.make_async_copy(s_in.at[at], held.at[at], sem.at[i]),
            pltpu.make_async_copy(held.at[at], s_out.at[at], sem.at[4 + i]),
        ))
        plain.append((
            pltpu.make_async_copy(p_in.at[at], held_p.at[at], sem.at[8 + i]),
            pltpu.make_async_copy(held_p.at[at], p_out.at[at], sem.at[12 + i]),
        ))
        parts[i][0].start()
    for i in range(4):
        plain[i][0].start()
    ahead = lax.broadcasted_iota(jnp.int32, (512, 512), 0)
    aside = lax.broadcasted_iota(jnp.int32, (512, 512), 1)
    back[...] = jnp.where(4 * lax.rem(ahead, 128) + ahead // 128 == aside, 1.0, 0.0).astype(jnp.bfloat16)
    for i in range(4):
        parts[i][0].wait()
        at = pl.ds(4 * i, 4)
        value = held[at].reshape(128, 512)
        held[at] = permuted(value, back[...], 3).reshape(4, 32, 512)
        parts[i][1].start()
        plain[i][0].wait()
        plain[i][1].start()
    for i in range(4):
        parts[i][1].wait()
        plain[i][1].wait()


def shards(rock, perm_tab, poro_tab, base, press, sat0, wells, well_rates):
    f32, i32 = jnp.float32, jnp.int32
    shape = jax.ShapeDtypeStruct(rock.shape, f32)
    hbm = pl.BlockSpec(memory_space=pl.ANY)
    smem = pl.BlockSpec(memory_space=pltpu.SMEM)
    vmem = pl.BlockSpec(memory_space=pltpu.VMEM)
    extended = pltpu.VMEM((4, EL, ER, 128), f32)
    block = pltpu.VMEM((LX, 32, 512), f32)
    halfway = pl.pallas_call(
        step_kernel,
        out_shape=(shape, shape),
        in_specs=[hbm, smem, smem, hbm, hbm, hbm, vmem, vmem],
        out_specs=(hbm, hbm),
        scratch_shapes=[
            pltpu.VMEM((EL, 24, 512), f32),
            pltpu.VMEM((EL, 24, 512), f32),
            pltpu.VMEM((NL, 24, 512), f32),
            pltpu.VMEM((NL, 16, 512), f32),
            pltpu.VMEM((LX, 32, 512), i32),
            block, block, block, block, block, block, block,
            pltpu.VMEM((2, 5, LX, 512), f32),
            pltpu.VMEM((2, 5, LX, 512), f32),
            pltpu.VMEM((2, LX, 512), f32),
            pltpu.VMEM((4, 2, 4, 16, 128), f32),
            pltpu.VMEM((5, NL, 512), f32),
            pltpu.VMEM((5, NL, 512), f32),
            pltpu.VMEM((NL, 512), f32),
            pltpu.VMEM((2, 2, 2, 4, 16, 128), f32),
            extended, extended, extended, extended, extended, extended, extended, extended, extended,
            pltpu.VMEM((4, EL + 1, 24, 128), f32),
            pltpu.VMEM((24 * (EL + 1), 2 * WELLS), jnp.bfloat16),
            pltpu.VMEM((512, 2 * WELLS), jnp.bfloat16),
            pltpu.VMEM((4, NL, 32, 128), f32),
            pltpu.VMEM((512, 512), jnp.bfloat16),
            pltpu.VMEM((512, 512), jnp.bfloat16),
            pltpu.VMEM((2, 2, 16, 128), f32),
            pltpu.VMEM((2, 2, 16, 128), f32),
            pltpu.VMEM((NL, 16, 512), f32),
            pltpu.VMEM((NL, 16, 512), f32),
            pltpu.SemaphoreType.DMA((12,)),
            pltpu.SemaphoreType.DMA((23,)),
            pltpu.SemaphoreType.DMA((20,)),
        ],
        compiler_params=pltpu.CompilerParams(
            collective_id=0, has_side_effects=True, vmem_limit_bytes=60 * 1024 * 1024
        ),
    )(rock, perm_tab, poro_tab, base, press, sat0, wells, well_rates.reshape(1, WELLS))
    return pl.pallas_call(
        finish_kernel,
        out_shape=(shape, shape),
        in_specs=[hbm, hbm],
        out_specs=(hbm, hbm),
        scratch_shapes=[block, block, pltpu.VMEM((512, 512), jnp.bfloat16), pltpu.SemaphoreType.DMA((16,))],
        compiler_params=pltpu.CompilerParams(vmem_limit_bytes=60 * 1024 * 1024),
    )(*halfway)


def solution(mesh):
    block = P("gx", "gy", None)
    return jax.shard_map(
        shards,
        mesh=mesh,
        in_specs=(block, P(), P(), block, block, block, P(), P()),
        out_specs=(block, block),
        check_vma=False,
    )
```

```python
import functools

import jax
import jax.numpy as jnp
from jax import lax
from jax.experimental import pallas as pl
from jax.experimental.pallas import tpu as pltpu
from jax.sharding import PartitionSpec as P

PASSES = 4
MOBILITY = 0.5
OMEGA = 0.8
VOLUME = 4.0
COMPRESS = 0.5

MESH = pl.DeviceIdType.MESH
LX = 16
NL = 32
EL = 41
LO = 4
ER = 40
RO = 12
ROCKS = 8
FAR = 1e30
NXC = 4
NGY = 16
WELLS = 512


def roll(value, shift):
    return pltpu.roll(value, shift % 128, 1)


def next_z(tiles):
    return [tiles[1], tiles[2], tiles[3], roll(tiles[0], -1)]


def prev_z(tiles):
    return [roll(tiles[3], 1), tiles[0], tiles[1], tiles[2]]


def layers(start, stop, block, body):
    whole = (stop - start) // block

    def several(i, _):
        for j in range(block):
            body(start + block * i + j)
        return 0

    lax.fori_loop(0, whole, several, 0)
    for l in range(start + block * whole, stop):
        body(l)


def recip(value):
    return pl.reciprocal(value, approx=False)


def permuted(value, matrix, parts):
    total, rest = None, value
    for k in range(parts):
        piece = rest.astype(jnp.bfloat16)
        term = jnp.dot(piece, matrix, preferred_element_type=jnp.float32)
        total = term if total is None else total + term
        if k < parts - 1:
            rest = rest - piece.astype(jnp.float32)
    return total


def lanes(z):
    return slice(128 * z, 128 * z + 128)


def step_kernel(
    rock, perm_tab, poro_tab, base, press, sat0, wells, well_rates,
    out_p, out_s,
    st_r, st_p, st_s, st_b,
    in_r, in_p, in_s, in_b, my_r, my_p, my_s, my_b, pk_r, pk_p, pk_s, pk_c, ys_r, ys_p, ys_s, co,
    hh, st, pa, pb, pc, te, tn, tb, ww, src, rt, hot_a, hot_b, fs, order, back,
    face_in, face_out, res_p, res_s,
    loc, snd, rcv,
):
    gx, gy = lax.axis_index("gx"), lax.axis_index("gy")
    xc, core = gx // 2, lax.rem(gx, 2)
    partner = (gx + 1 - 2 * core, gy)
    low, high = xc > 0, xc < NXC - 1
    down, up = gy > 0, gy < NGY - 1
    f32 = jnp.float32

    barrier = pltpu.get_barrier_semaphore()
    outer = ((core == 0) & down) | ((core == 1) & up)
    outer_y = gy - 1 + 2 * core

    def greet(ok, device):
        def signal():
            pl.semaphore_signal(barrier, inc=1, device_id=device, device_id_type=MESH)

        signal() if ok is None else pl.when(ok)(signal)

    greet(None, partner)
    greet(low, (2 * xc - 1, gy))
    greet(high, (2 * xc + 2, gy))
    greet(low & (core == 0), (2 * xc - 2, gy))
    greet(outer, (2 * xc, outer_y))
    greet(outer, (2 * xc + 1, outer_y))
    greet(outer & low, (2 * xc - 1, outer_y))
    greet(outer & high, (2 * xc + 2, outer_y))
    one = lambda ok: ok.astype(jnp.int32)
    beside = jnp.where(core == 0, one(low), one(high))
    across = one(down) + one(up)
    count = 1 + 2 * beside + one(high & (core == 0)) + across * (1 + beside)

    def local(k, a, b):
        return pltpu.make_async_copy(a, b, loc.at[k])

    row24 = pl.ds(pl.multiple_of(8 * core, 8), 24)
    row16 = pl.ds(pl.multiple_of(16 * core, 16), 16)
    own = pl.ds(LO + LX * core, LX)
    own0 = pl.ds(LX * core, LX)
    loads = [
        local(0, rock, in_r), local(1, press, in_p), local(2, sat0, in_s), local(3, base, in_b)
    ]
    for copy in loads:
        copy.start()
    blocks = [
        local(4, my_r.at[:, row24, :], st_r.at[own]),
        local(5, my_p.at[:, row24, :], st_p.at[own]),
        local(6, my_s.at[:, row24, :], st_s.at[own0]),
        local(7, my_b.at[:, row16, :], st_b.at[own0]),
    ]

    def remote(k, j, a, b, device):
        return pltpu.make_async_remote_copy(
            src_ref=a, dst_ref=b, send_sem=snd.at[k], recv_sem=rcv.at[j], device_id=device, device_id_type=MESH
        )

    other24 = pl.ds(pl.multiple_of(8 * (1 - core), 8), 24)
    other16 = pl.ds(pl.multiple_of(16 * (1 - core), 16), 16)
    sends = []
    ypart = pl.ds(pl.multiple_of(LX * core, 16), LX)
    last_layers, first_layers = (core == 1) & high, (core == 0) & low
    for k, (a, b, pk, ys) in enumerate(((my_r, st_r, pk_r, ys_r), (my_p, st_p, pk_p, ys_p))):
        for side, ok, device in ((0, down, (2 * xc + 1, gy - 1)), (1, up, (2 * xc, gy + 1))):
            sends.append((ok, remote(4 + 2 * k + side, 4 + k, pk.at[side], ys.at[:, ypart, :], device)))
        for d in (0, 1):
            rows, place = pl.ds(16 * d, 16), pl.ds(8 * d, 16)
            sends.append((last_layers, remote(
                8 + 2 * d + k, 7 + k, a.at[pl.ds(12, 4), rows, :], b.at[pl.ds(0, 4), place, :], (2 * (xc + 1) + d, gy),
            )))
            sends.append((first_layers, remote(
                8 + 2 * d + k, 9 + k, a.at[pl.ds(0, 5), rows, :], b.at[pl.ds(LO + NL, 5), place, :], (2 * (xc - 1) + d, gy),
            )))
        sends.append((None, remote(k, k, a.at[:, other24, :], b.at[own], partner)))
    for group, (ok, d, dy, kind) in enumerate(((down, 1, -1, 0), (up, 0, 1, 0), (None, 1, 0, 1), (None, 0, 0, 1))):
        for part, side, dx in ((last_layers, 0, 1), (first_layers, 1, -1)):
            sends.append((
                part if ok is None else part & ok,
                remote(12 + group, 11 + 2 * kind + side, pk_c.at[group], co.at[kind, side], (2 * (xc + dx) + d, gy + dy)),
            ))
    sends_late = []
    for side, ok, device in ((0, down, (2 * xc + 1, gy - 1)), (1, up, (2 * xc, gy + 1))):
        sends_late.append((ok, remote(16 + side, 6, pk_s.at[side], ys_s.at[ypart, :], device)))
    sends_late.append((None, remote(2, 2, my_s.at[:, other24, :], st_s.at[own0], partner)))
    sends_late.append((None, remote(3, 3, my_b.at[:, other16, :], st_b.at[own0], partner)))

    def guarded(ok, action):
        if ok is None:
            action()
        else:
            pl.when(ok)(action)

    def arrived(k, ref, ok=None):
        guarded(ok, lambda: pltpu.make_async_copy(ref, ref, rcv.at[k]).wait())

    outer = ((core == 0) & down) | ((core == 1) & up)

    def depth_of(place):
        return 4 * lax.rem(place, 128) + place // 128

    ahead = lax.broadcasted_iota(jnp.int32, (512, 512), 0)
    aside = lax.broadcasted_iota(jnp.int32, (512, 512), 1)
    order[...] = jnp.where(ahead == depth_of(aside), 1.0, 0.0).astype(jnp.bfloat16)
    back[...] = jnp.where(depth_of(ahead) == aside, 1.0, 0.0).astype(jnp.bfloat16)

    def reorder(a, b, parts):
        def body(m, _):
            at = pl.ds(pl.multiple_of(8 * m, 8), 8)
            value = a[at].reshape(256, 512).astype(f32)
            b[at] = permuted(value, order[...], parts).reshape(8, 32, 512)
            return 0

        lax.fori_loop(0, 2, body, 0)

    loads[0].wait()
    reorder(in_r, my_r, 1)
    loads[1].wait()
    reorder(in_p, my_p, 3)
    for side in (0, 1):
        for a, b in ((my_r, pk_r), (my_p, pk_p)):
            for r in range(5):
                b[side, r] = a[:, r + 27 * side, :]

    def by_core(action):
        for c in (0, 1):
            pl.when(core == c)(functools.partial(action, c))

    def pack_corners(c):
        part = slice(12, 16) if c == 1 else slice(0, 4)
        for group, row in enumerate((0, 28, 12, 16)):
            for k, a in enumerate((my_r, my_p)):
                for r in range(4):
                    for z in range(4):
                        pk_c[group, k, r, 4 * z : 4 * z + 4, :] = a[part, row + r, lanes(z)]

    by_core(pack_corners)
    blocks[0].start()
    blocks[1].start()
    pl.semaphore_wait(barrier, count)
    for ok, copy in sends:
        guarded(ok, copy.start)
    loads[2].wait()
    reorder(in_s, my_s, 3)
    for side in (0, 1):
        pk_s[side] = my_s[:, 31 * side, :]
    loads[3].wait()
    reorder(in_b, my_b, 3)
    blocks[2].start()
    blocks[3].start()
    for ok, copy in sends_late:
        guarded(ok, copy.start)

    @pl.when(jnp.logical_not(low))
    def _():
        st_r[0:LO] = jnp.full((LO, 24, 512), float(ROCKS), f32)
        st_p[0:LO] = jnp.zeros((LO, 24, 512), f32)

    @pl.when(jnp.logical_not(high))
    def _():
        st_r[LO + NL :] = jnp.full((5, 24, 512), float(ROCKS), f32)
        st_p[LO + NL :] = jnp.zeros((5, 24, 512), f32)

    @pl.when(jnp.logical_not(outer))
    def _():
        ys_r[...] = jnp.full((5, NL, 512), float(ROCKS), f32)
        ys_p[...] = jnp.zeros((5, NL, 512), f32)
        ys_s[...] = jnp.zeros((NL, 512), f32)

    for side, ok in ((0, low), (1, high)):

        @pl.when(jnp.logical_not(ok & outer))
        def _(side=side):
            co[0, side, 0] = jnp.full((4, 16, 128), float(ROCKS), f32)
            co[0, side, 1] = jnp.zeros((4, 16, 128), f32)

        @pl.when(jnp.logical_not(ok))
        def _(side=side):
            co[1, side, 0] = jnp.full((4, 16, 128), float(ROCKS), f32)
            co[1, side, 1] = jnp.zeros((4, 16, 128), f32)

    well_x, well_y, well_z = wells[0:1, :], wells[1:2, :], wells[2:3, :]
    rate = well_rates[...]
    x0, y0 = NL * xc - LO, NL * gy + LX * core - 4
    columns = depth_of(lax.broadcasted_iota(jnp.int32, (512, WELLS), 0))
    one_z = jnp.where(columns == well_z, 1.0, 0.0).astype(jnp.bfloat16)
    hot_b[:, 0:WELLS] = one_z
    hot_b[:, WELLS:] = one_z
    pair_ids = lax.broadcasted_iota(jnp.int32, (48, WELLS), 0)
    second = pair_ids >= 24
    row_ids = jnp.where(second, pair_ids - 24, pair_ids) + y0
    layer_ids = jnp.where(second, 1, 0) + x0
    high_part = rate.astype(jnp.bfloat16).astype(f32)
    low_part = rate - high_part

    def hot_rows(l, _):
        here = (row_ids == well_y) & (layer_ids == well_x - 2 * l)
        at = pl.ds(pl.multiple_of(48 * l, 16), 48)
        hot_a[at, 0:WELLS] = jnp.where(here, high_part, 0.0).astype(jnp.bfloat16)
        hot_a[at, WELLS:] = jnp.where(here, low_part, 0.0).astype(jnp.bfloat16)
        return 0

    lax.fori_loop(0, (EL + 1) // 2, hot_rows, 0)

    def spread(m, _):
        at = pl.ds(pl.multiple_of(336 * m, 16), 336)
        got = lax.dot_general(
            hot_a[at, :], hot_b[...], (((1,), (1,)), ((), ())), preferred_element_type=f32
        )
        for z in range(4):
            rt[z, pl.ds(14 * m, 14)] = got[:, lanes(z)].reshape(14, 24, 128)
        return 0

    lax.fori_loop(0, 3, spread, 0)

    def table(ref, rule):
        return [rule(jnp.full((8, 128), ref[k], f32)) for k in range(ROCKS)]

    tab_h = table(perm_tab, lambda v: 0.5 / v) + [jnp.full((8, 128), FAR, f32)]
    tab_s = table(poro_tab, lambda v: (COMPRESS * VOLUME) * v) + [jnp.full((8, 128), 1.0, f32)]

    def lookup(kinds, n=8):
        h, s = tab_h[0][:n], tab_s[0][:n]
        for k in range(1, ROCKS + 1):
            later = kinds > k - 0.5
            h = jnp.where(later, tab_h[k][:n], h)
            s = jnp.where(later, tab_s[k][:n], s)
        return h, s

    def unpack_layers(first, last, at_row, tiles=(0, 1, 2)):
        def body(l, _):
            for z in range(4):
                for t in tiles:
                    h, s = lookup(st_r[l, 8 * t : 8 * t + 8, lanes(z)])
                    e = at_row + 8 * t
                    hh[z, l, e : e + 8, :] = h
                    st[z, l, e : e + 8, :] = s
                    pa[z, l, e : e + 8, :] = st_p[l, 8 * t : 8 * t + 8, lanes(z)]
            return 0

        lax.fori_loop(first, last, body, 0)

    for copy in blocks:
        copy.wait()
    arrived(0, st_r.at[pl.ds(LO, LX)])
    arrived(1, st_p.at[pl.ds(LO, LX)])
    by_core(lambda c: unpack_layers(LO, LO + NL, RO - 8 * c))

    def side_faces(l, e0=8, e1=32, n0=0, n1=32):
        for z in range(4):
            te[z, l, e0:e1, :] = recip(hh[z, l, e0:e1, :] + hh[z, l + 1, e0:e1, :])
            tn[z, l, n0:n1, :] = recip(hh[z, l, n0:n1, :] + hh[z, l, n0 + 1 : n1 + 1, :])

    def weights(l, e0=8, e1=32):
        own_h = [hh[z, l, e0:e1, :] for z in range(4)]
        deeper = next_z(own_h)
        below = [recip(own_h[z] + deeper[z]) for z in range(4)]
        last = lax.broadcasted_iota(jnp.int32, (e1 - e0, 128), 1) == 127
        below[3] = jnp.where(last, 0.0, below[3])
        above = prev_z(below)
        for z in (1, 2, 3, 0):
            tb[z, l, e0:e1, :] = below[z]
            storage = st[z, l, e0:e1, :]
            diagonal = (
                storage + te[z, l, e0:e1, :] + te[z, l - 1, e0:e1, :]
                + tn[z, l, e0:e1, :] + tn[z, l, e0 - 1 : e1 - 1, :] + below[z] + above[z]
            )
            ww[z, l, e0:e1, :] = OMEGA * recip(diagonal)
            src[z, l, e0:e1, :] = storage * pa[z, l, e0:e1, :] + rt[z, l, e0 - 8 : e1 - 8, :]

    def one_pass(old, new, start, stop, block, e0=8, e1=32):
        def body(l):
            here = [old[z, l, e0:e1, :] for z in range(4)]
            faces = [tb[z, l, e0:e1, :] for z in range(4)]
            deeper = next_z(here)
            shallower = prev_z([faces[z] * here[z] for z in range(4)])
            for z in (1, 2, 3, 0):
                total = (
                    src[z, l, e0:e1, :] + faces[z] * deeper[z] + shallower[z]
                    + te[z, l, e0:e1, :] * old[z, l + 1, e0:e1, :]
                    + te[z, l - 1, e0:e1, :] * old[z, l - 1, e0:e1, :]
                    + tn[z, l, e0:e1, :] * old[z, l, e0 + 1 : e1 + 1, :]
                    + tn[z, l, e0 - 1 : e1 - 1, :] * old[z, l, e0 - 1 : e1 - 1, :]
                )
                new[z, l, e0:e1, :] = (1.0 - OMEGA) * here[z] + ww[z, l, e0:e1, :] * total

        layers(start, stop, block, body)

    layers(LO, LO + NL - 1, 4, side_faces)
    layers(5, 35, 3, weights)
    one_pass(pa, pb, 5, 35, 3)
    one_pass(pb, pc, 6, 34, 4)

    def fraction(s):
        q = s * s
        return q * recip(1.5 * q + (0.5 - s))

    arrived(2, st_s.at[pl.ds(0, LX)])
    arrived(3, st_b.at[pl.ds(0, LX)])

    def unpack_fraction(c):
        def body(l, _):
            for z in range(4):
                for t in range(3):
                    e = 8 - 8 * c + 8 * t
                    fs[z, l, e : e + 8, :] = fraction(st_s[l, 8 * t : 8 * t + 8, lanes(z)])
            return 0

        lax.fori_loop(0, NL, body, 0)

    by_core(unpack_fraction)

    arrived(4, ys_r, outer)
    arrived(5, ys_p, outer)
    arrived(6, ys_s, outer)
    rows_here = pl.ds(pl.multiple_of(8 * core, 8), 16)
    arrived(7, st_r.at[pl.ds(0, 4), rows_here, :], low)
    arrived(8, st_p.at[pl.ds(0, 4), rows_here, :], low)
    arrived(9, st_r.at[pl.ds(LO + NL, 5), rows_here, :], high)
    arrived(10, st_p.at[pl.ds(LO + NL, 5), rows_here, :], high)
    arrived(11, co.at[0, 0], low & outer)
    arrived(12, co.at[0, 1], high & outer)
    arrived(13, co.at[1, 0], low)
    arrived(14, co.at[1, 1], high)

    def unpack_halo(c):
        unpack_layers(0, LO, RO - 8 * c, (c, c + 1))
        unpack_layers(LO + NL, EL, RO - 8 * c, (c, c + 1))
        e = 7 if c == 0 else 28

        for z in range(4):
            for r in range(5):
                for g in range(4):
                    at = pl.ds(LO + 8 * g, 8)
                    h, s = lookup(ys_r[r, 8 * g : 8 * g + 8, lanes(z)])
                    hh[z, at, e + r, :] = h
                    st[z, at, e + r, :] = s
                    pa[z, at, e + r, :] = ys_p[r, 8 * g : 8 * g + 8, lanes(z)]
            for kind in (0, 1):
                e4 = 8 if c == kind else 28
                for r in range(4):
                    for side, place in ((0, 0), (1, LO + NL)):
                        at = pl.ds(place, 4)
                        h, s = lookup(co[kind, side, 0, r, 4 * z : 4 * z + 4, :], 4)
                        hh[z, at, e4 + r, :] = h
                        st[z, at, e4 + r, :] = s
                        pa[z, at, e4 + r, :] = co[kind, side, 1, r, 4 * z : 4 * z + 4, :]
            fs[z, :, 7 if c == 0 else 24, :] = fraction(ys_s[:, lanes(z)])

    by_core(unpack_halo)

    def finish_passes(c):
        e0, e1 = (8, 16) if c == 0 else (24, 32)
        n0 = 0 if c == 0 else 24
        layers(0, LO, 2, side_faces)
        layers(LO + NL - 1, EL - 1, 2, side_faces)
        layers(LO, LO + NL - 1, 4, lambda l: side_faces(l, e0, e1, n0, e1))
        layers(1, 5, 4, weights)
        layers(35, 40, 5, weights)
        layers(5, 35, 6, lambda l: weights(l, e0, e1))
        one_pass(pa, pb, 1, 5, 4)
        one_pass(pa, pb, 35, 40, 5)
        one_pass(pa, pb, 5, 35, 6, e0, e1)
        one_pass(pb, pc, 2, 6, 4)
        one_pass(pb, pc, 34, 39, 5)
        one_pass(pb, pc, 6, 34, 7, e0, e1)

    by_core(finish_passes)
    one_pass(pc, pa, 3, 38, 4)
    one_pass(pa, pb, 4, 37, 4)

    def fluxes(l):
        e = l + LO
        center = [pb[z, e, RO : RO + 16, :] for z in range(4)]
        frac = [fs[z, l, 8:24, :] for z in range(4)]
        deeper, frac_deep = next_z(center), next_z(frac)
        drained = []
        for z in range(4):
            flow = tb[z, e, RO : RO + 16, :] * (center[z] - deeper[z])
            drained.append(flow * jnp.where(flow > 0, frac[z], frac_deep[z]))
        entered = prev_z(drained)
        at = pl.ds(pl.multiple_of(8 * core, 8), 16)
        for z in range(4):
            p, f = center[z], frac[z]
            res_p[l, :, lanes(z)] = p
            through = jnp.maximum(
                st_b[l, :, lanes(z)] + te[z, e, RO : RO + 16, :] * (p - pb[z, e + 1, RO : RO + 16, :]), 0.0
            )
            north = tn[z, e, RO : RO + 16, :] * (p - pb[z, e, RO + 1 : RO + 17, :])
            south = tn[z, e, RO - 1 : RO + 15, :] * (p - pb[z, e, RO - 1 : RO + 15, :])
            leaving = drained[z] - entered[z]
            leaving = leaving + north * jnp.where(north > 0, f, fs[z, l, 9:25, :])
            leaving = leaving + south * jnp.where(south > 0, f, fs[z, l, 7:23, :])
            rates = rt[z, e, 4:20, :]
            extra = rates * jnp.where(rates > 0, 1.0, f) - leaving
            per_volume = recip((1.0 / COMPRESS) * st[z, e, RO : RO + 16, :])
            s = st_s[l, at, lanes(z)]
            q = s * s
            inverse = recip(1.5 * q + (0.5 - s))
            slope = (s - q) * inverse * inverse
            extra = extra * per_volume
            relative = through * per_volume
            step = recip(1.0 + relative * slope)
            hh[z, l, 8:24, :] = s + extra
            hh[z, l, 24:40, :] = per_volume
            pc[z, l, 8:24, :] = s + (extra - relative * f) * step
            pc[z, l, 24:40, :] = per_volume * step
            ww[z, l, 8:24, :] = relative
            ww[z, l, 24:40, :] = through

    layers(0, NL, 2, fluxes)

    theirs = pl.ds(LX * (1 - core), LX)
    out_rows = pl.ds(pl.multiple_of(16 * core, 16), 16)
    keep_p = local(8, res_p.at[own0], out_p.at[:, out_rows, :])
    give_p = remote(18, 15, res_p.at[theirs], out_p.at[:, out_rows, :], partner)

    def restore(ref, first, count):
        at = pl.ds(first, count)
        value = ref[at].reshape(16 * count, 512)
        ref[at] = permuted(value, back[...], 3).reshape(count, 16, 512)

    def hand_back_pressure():
        for first in (0, 16):
            restore(res_p, first, 16)
        keep_p.start()
        give_p.start()

    pl.when(low)(hand_back_pressure)

    def newton(s, c, relative):
        q = s * s
        d = 1.5 * q + (0.5 - s)
        return d * d + relative * (s - q), d * (d * (s - c) + relative * q)

    waves, keeps, gives = [], [], []
    for half in (0, 1):
        tiles = (2 * half, 2 * half + 1)
        wide = pl.ds(256 * half, 256)
        waves.append(remote(19 + half, 16 + half, face_out.at[half], face_in.at[half], (gx + 2, gy)))
        keeps.append(local(10 + half, res_s.at[own0, :, wide], out_s.at[:, out_rows, wide]))
        gives.append(remote(21 + half, 18 + half, res_s.at[theirs, :, wide], out_s.at[:, out_rows, wide], partner))

        @pl.when(jnp.logical_not(low))
        def _(half=half, tiles=tiles):
            for z in tiles:
                face_in[half, z % 2] = st_b[0, :, lanes(z)]

        arrived(16 + half, face_in.at[half], low)

        def sweep(l, coming, tiles=tiles):
            going = []
            for z in tiles:
                relative = ww[z, l, 8:24, :]
                inflow = coming[z % 2]
                c = hh[z, l, 8:24, :] + hh[z, l, 24:40, :] * inflow
                s = jnp.clip(pc[z, l, 8:24, :] + pc[z, l, 24:40, :] * inflow, 0.0, 1.0)
                below, above = newton(s, c, relative)
                s = jnp.clip(s - above * recip(below), 0.0, 1.0)
                below, above = newton(s, c, relative)
                top = jnp.minimum(jnp.maximum(s * below - above, 0.0), below)
                res_s[l, :, lanes(z)] = top * recip(below)
                rest = (below - top) * (MOBILITY**0.5)
                top = top * top
                going.append(ww[z, l, 24:40, :] * top * recip(top + rest * rest))
            return going

        coming = lax.fori_loop(0, NL, sweep, [face_in[half, 0], face_in[half, 1]], unroll=4)
        for z in (0, 1):
            face_out[half, z] = coming[z]
        pl.when(high)(waves[half].start)
        keeps[half].start()
        gives[half].start()

    pl.when(jnp.logical_not(low))(hand_back_pressure)

    for ok, copy in sends + sends_late:
        guarded(ok, copy.wait_send)
    keep_p.wait()
    give_p.wait()
    for half in (0, 1):
        keeps[half].wait()
        pl.when(high)(waves[half].wait_send)
        gives[half].wait()


def finish_kernel(p_in, s_in, p_out, s_out, held_p, held, back, sem):
    parts, plain = [], []
    for i in range(4):
        at = pl.ds(4 * i, 4)
        parts.append((
            pltpu.make_async_copy(s_in.at[at], held.at[at], sem.at[i]),
            pltpu.make_async_copy(held.at[at], s_out.at[at], sem.at[4 + i]),
        ))
        plain.append((
            pltpu.make_async_copy(p_in.at[at], held_p.at[at], sem.at[8 + i]),
            pltpu.make_async_copy(held_p.at[at], p_out.at[at], sem.at[12 + i]),
        ))
        parts[i][0].start()
    for i in range(4):
        plain[i][0].start()
    ahead = lax.broadcasted_iota(jnp.int32, (512, 512), 0)
    aside = lax.broadcasted_iota(jnp.int32, (512, 512), 1)
    back[...] = jnp.where(4 * lax.rem(ahead, 128) + ahead // 128 == aside, 1.0, 0.0).astype(jnp.bfloat16)
    for i in range(4):
        parts[i][0].wait()
        at = pl.ds(4 * i, 4)
        value = held[at].reshape(128, 512)
        held[at] = permuted(value, back[...], 3).reshape(4, 32, 512)
        parts[i][1].start()
        plain[i][0].wait()
        plain[i][1].start()
    for i in range(4):
        parts[i][1].wait()
        plain[i][1].wait()


def shards(rock, perm_tab, poro_tab, base, press, sat0, wells, well_rates):
    f32, i32 = jnp.float32, jnp.int32
    shape = jax.ShapeDtypeStruct(rock.shape, f32)
    hbm = pl.BlockSpec(memory_space=pl.ANY)
    smem = pl.BlockSpec(memory_space=pltpu.SMEM)
    vmem = pl.BlockSpec(memory_space=pltpu.VMEM)
    extended = pltpu.VMEM((4, EL, ER, 128), f32)
    block = pltpu.VMEM((LX, 32, 512), f32)
    halfway = pl.pallas_call(
        step_kernel,
        out_shape=(shape, shape),
        in_specs=[hbm, smem, smem, hbm, hbm, hbm, vmem, vmem],
        out_specs=(hbm, hbm),
        scratch_shapes=[
            pltpu.VMEM((EL, 24, 512), f32),
            pltpu.VMEM((EL, 24, 512), f32),
            pltpu.VMEM((NL, 24, 512), f32),
            pltpu.VMEM((NL, 16, 512), f32),
            pltpu.VMEM((LX, 32, 512), i32),
            block, block, block, block, block, block, block,
            pltpu.VMEM((2, 5, LX, 512), f32),
            pltpu.VMEM((2, 5, LX, 512), f32),
            pltpu.VMEM((2, LX, 512), f32),
            pltpu.VMEM((4, 2, 4, 16, 128), f32),
            pltpu.VMEM((5, NL, 512), f32),
            pltpu.VMEM((5, NL, 512), f32),
            pltpu.VMEM((NL, 512), f32),
            pltpu.VMEM((2, 2, 2, 4, 16, 128), f32),
            extended, extended, extended, extended, extended, extended, extended, extended, extended, extended,
            pltpu.VMEM((4, EL + 1, 24, 128), f32),
            pltpu.VMEM((24 * (EL + 1), 2 * WELLS), jnp.bfloat16),
            pltpu.VMEM((512, 2 * WELLS), jnp.bfloat16),
            pltpu.VMEM((4, NL, 32, 128), f32),
            pltpu.VMEM((512, 512), jnp.bfloat16),
            pltpu.VMEM((512, 512), jnp.bfloat16),
            pltpu.VMEM((2, 2, 16, 128), f32),
            pltpu.VMEM((2, 2, 16, 128), f32),
            pltpu.VMEM((NL, 16, 512), f32),
            pltpu.VMEM((NL, 16, 512), f32),
            pltpu.SemaphoreType.DMA((12,)),
            pltpu.SemaphoreType.DMA((23,)),
            pltpu.SemaphoreType.DMA((20,)),
        ],
        compiler_params=pltpu.CompilerParams(
            collective_id=0, has_side_effects=True, vmem_limit_bytes=60 * 1024 * 1024
        ),
    )(rock, perm_tab, poro_tab, base, press, sat0, wells, well_rates.reshape(1, WELLS))
    return pl.pallas_call(
        finish_kernel,
        out_shape=(shape, shape),
        in_specs=[hbm, hbm],
        out_specs=(hbm, hbm),
        scratch_shapes=[block, block, pltpu.VMEM((512, 512), jnp.bfloat16), pltpu.SemaphoreType.DMA((16,))],
        compiler_params=pltpu.CompilerParams(vmem_limit_bytes=60 * 1024 * 1024),
    )(*halfway)


def solution(mesh):
    block = P("gx", "gy", None)
    return jax.shard_map(
        shards,
        mesh=mesh,
        in_specs=(block, P(), P(), block, block, block, P(), P()),
        out_specs=(block, block),
        check_vma=False,
    )
```

```python
import functools

import jax
import jax.numpy as jnp
from jax import lax
from jax.experimental import pallas as pl
from jax.experimental.pallas import tpu as pltpu
from jax.sharding import PartitionSpec as P

PASSES = 4
MOBILITY = 0.5
OMEGA = 0.8
VOLUME = 4.0
COMPRESS = 0.5

MESH = pl.DeviceIdType.MESH
LX = 16
NL = 32
EL = 41
LO = 4
ER = 40
RO = 12
ROCKS = 8
FAR = 1e30
NXC = 4
NGY = 16
WELLS = 512


def roll(value, shift):
    return pltpu.roll(value, shift % 128, 1)


def next_z(tiles):
    return [tiles[1], tiles[2], tiles[3], roll(tiles[0], -1)]


def prev_z(tiles):
    return [roll(tiles[3], 1), tiles[0], tiles[1], tiles[2]]


def layers(start, stop, block, body):
    whole = (stop - start) // block

    def several(i, _):
        for j in range(block):
            body(start + block * i + j)
        return 0

    lax.fori_loop(0, whole, several, 0)
    for l in range(start + block * whole, stop):
        body(l)


def recip(value):
    return pl.reciprocal(value, approx=False)


def permuted(value, matrix, parts):
    total, rest = None, value
    for k in range(parts):
        piece = rest.astype(jnp.bfloat16)
        term = jnp.dot(piece, matrix, preferred_element_type=jnp.float32)
        total = term if total is None else total + term
        if k < parts - 1:
            rest = rest - piece.astype(jnp.float32)
    return total


def lanes(z):
    return slice(128 * z, 128 * z + 128)


def step_kernel(
    rock, perm_tab, poro_tab, base, press, sat0, wells, well_rates,
    out_p, out_s,
    st_r, st_p, st_s, st_b,
    in_r, my_r, my_p, my_s, my_b, pk_r, pk_p, pk_s, pk_c, ys_r, ys_p, ys_s, co,
    hh, st, pa, pb, pc, pd, te, tn, tb, ww, src, rt, hot_a, hot_b, fs, order, back,
    face_in, face_out, res_p, res_s,
    loc, snd, rcv,
):
    gx, gy = lax.axis_index("gx"), lax.axis_index("gy")
    xc, core = gx // 2, lax.rem(gx, 2)
    partner = (gx + 1 - 2 * core, gy)
    low, high = xc > 0, xc < NXC - 1
    down, up = gy > 0, gy < NGY - 1
    f32 = jnp.float32

    barrier = pltpu.get_barrier_semaphore()
    outer = ((core == 0) & down) | ((core == 1) & up)
    outer_y = gy - 1 + 2 * core

    def greet(ok, device):
        def signal():
            pl.semaphore_signal(barrier, inc=1, device_id=device, device_id_type=MESH)

        signal() if ok is None else pl.when(ok)(signal)

    greet(None, partner)
    greet(low, (2 * xc - 1, gy))
    greet(high, (2 * xc + 2, gy))
    greet(low & (core == 0), (2 * xc - 2, gy))
    greet(outer, (2 * xc, outer_y))
    greet(outer, (2 * xc + 1, outer_y))
    greet(outer & low, (2 * xc - 1, outer_y))
    greet(outer & high, (2 * xc + 2, outer_y))
    one = lambda ok: ok.astype(jnp.int32)
    beside = jnp.where(core == 0, one(low), one(high))
    across = one(down) + one(up)
    count = 1 + 2 * beside + one(high & (core == 0)) + across * (1 + beside)

    def local(k, a, b):
        return pltpu.make_async_copy(a, b, loc.at[k])

    row24 = pl.ds(pl.multiple_of(8 * core, 8), 24)
    row16 = pl.ds(pl.multiple_of(16 * core, 16), 16)
    own = pl.ds(LO + LX * core, LX)
    own0 = pl.ds(LX * core, LX)
    loads = [
        local(0, rock, in_r), local(1, press, my_p), local(2, sat0, my_s), local(3, base, my_b)
    ]
    for copy in loads:
        copy.start()
    blocks = [
        local(4, my_r.at[:, row24, :], st_r.at[own]),
        local(5, my_p.at[:, row24, :], st_p.at[own]),
        local(6, my_s.at[:, row24, :], st_s.at[own0]),
        local(7, my_b.at[:, row16, :], st_b.at[own0]),
    ]

    def remote(k, j, a, b, device):
        return pltpu.make_async_remote_copy(
            src_ref=a, dst_ref=b, send_sem=snd.at[k], recv_sem=rcv.at[j], device_id=device, device_id_type=MESH
        )

    other24 = pl.ds(pl.multiple_of(8 * (1 - core), 8), 24)
    other16 = pl.ds(pl.multiple_of(16 * (1 - core), 16), 16)
    sends = []
    ypart = pl.ds(pl.multiple_of(LX * core, 16), LX)
    last_layers, first_layers = (core == 1) & high, (core == 0) & low
    for k, (a, b, pk, ys) in enumerate(((my_r, st_r, pk_r, ys_r), (my_p, st_p, pk_p, ys_p))):
        for side, ok, device in ((0, down, (2 * xc + 1, gy - 1)), (1, up, (2 * xc, gy + 1))):
            sends.append((ok, remote(4 + 2 * k + side, 4 + k, pk.at[side], ys.at[:, ypart, :], device)))
        for d in (0, 1):
            rows, place = pl.ds(16 * d, 16), pl.ds(8 * d, 16)
            sends.append((last_layers, remote(
                8 + 2 * d + k, 7 + k, a.at[pl.ds(12, 4), rows, :], b.at[pl.ds(0, 4), place, :], (2 * (xc + 1) + d, gy),
            )))
            sends.append((first_layers, remote(
                8 + 2 * d + k, 9 + k, a.at[pl.ds(0, 5), rows, :], b.at[pl.ds(LO + NL, 5), place, :], (2 * (xc - 1) + d, gy),
            )))
        sends.append((None, remote(k, k, a.at[:, other24, :], b.at[own], partner)))
    for group, (ok, d, dy, kind) in enumerate(((down, 1, -1, 0), (up, 0, 1, 0), (None, 1, 0, 1), (None, 0, 0, 1))):
        for part, side, dx in ((last_layers, 0, 1), (first_layers, 1, -1)):
            sends.append((
                part if ok is None else part & ok,
                remote(12 + group, 11 + 2 * kind + side, pk_c.at[group], co.at[kind, side], (2 * (xc + dx) + d, gy + dy)),
            ))
    sends_late = []
    for side, ok, device in ((0, down, (2 * xc + 1, gy - 1)), (1, up, (2 * xc, gy + 1))):
        sends_late.append((ok, remote(16 + side, 6, pk_s.at[side], ys_s.at[ypart, :], device)))
    sends_late.append((None, remote(2, 2, my_s.at[:, other24, :], st_s.at[own0], partner)))
    sends_late.append((None, remote(3, 3, my_b.at[:, other16, :], st_b.at[own0], partner)))

    def guarded(ok, action):
        if ok is None:
            action()
        else:
            pl.when(ok)(action)

    def arrived(k, ref, ok=None):
        guarded(ok, lambda: pltpu.make_async_copy(ref, ref, rcv.at[k]).wait())

    outer = ((core == 0) & down) | ((core == 1) & up)

    def depth_of(place):
        return 4 * lax.rem(place, 128) + place // 128

    ahead = lax.broadcasted_iota(jnp.int32, (512, 512), 0)
    aside = lax.broadcasted_iota(jnp.int32, (512, 512), 1)
    order[...] = jnp.where(ahead == depth_of(aside), 1.0, 0.0).astype(jnp.bfloat16)
    back[...] = jnp.where(depth_of(ahead) == aside, 1.0, 0.0).astype(jnp.bfloat16)

    def reorder(a, b, parts):
        def body(m, _):
            at = pl.ds(pl.multiple_of(8 * m, 8), 8)
            value = a[at].reshape(256, 512).astype(f32)
            b[at] = permuted(value, order[...], parts).reshape(8, 32, 512)
            return 0

        lax.fori_loop(0, 2, body, 0)

    loads[0].wait()
    reorder(in_r, my_r, 1)
    loads[1].wait()
    reorder(my_p, my_p, 3)
    for side in (0, 1):
        for a, b in ((my_r, pk_r), (my_p, pk_p)):
            for r in range(5):
                b[side, r] = a[:, r + 27 * side, :]

    def by_core(action):
        for c in (0, 1):
            pl.when(core == c)(functools.partial(action, c))

    def pack_corners(c):
        part = slice(12, 16) if c == 1 else slice(0, 4)
        for group, row in enumerate((0, 28, 12, 16)):
            for k, a in enumerate((my_r, my_p)):
                for r in range(4):
                    for z in range(4):
                        pk_c[group, k, r, 4 * z : 4 * z + 4, :] = a[part, row + r, lanes(z)]

    by_core(pack_corners)
    blocks[0].start()
    blocks[1].start()
    pl.semaphore_wait(barrier, count)
    for ok, copy in sends:
        guarded(ok, copy.start)
    loads[2].wait()
    reorder(my_s, my_s, 3)
    for side in (0, 1):
        pk_s[side] = my_s[:, 31 * side, :]
    loads[3].wait()
    reorder(my_b, my_b, 3)
    blocks[2].start()
    blocks[3].start()
    for ok, copy in sends_late:
        guarded(ok, copy.start)

    @pl.when(jnp.logical_not(low))
    def _():
        st_r[0:LO] = jnp.full((LO, 24, 512), float(ROCKS), f32)
        st_p[0:LO] = jnp.zeros((LO, 24, 512), f32)

    @pl.when(jnp.logical_not(high))
    def _():
        st_r[LO + NL :] = jnp.full((5, 24, 512), float(ROCKS), f32)
        st_p[LO + NL :] = jnp.zeros((5, 24, 512), f32)

    @pl.when(jnp.logical_not(outer))
    def _():
        ys_r[...] = jnp.full((5, NL, 512), float(ROCKS), f32)
        ys_p[...] = jnp.zeros((5, NL, 512), f32)
        ys_s[...] = jnp.zeros((NL, 512), f32)

    for side, ok in ((0, low), (1, high)):

        @pl.when(jnp.logical_not(ok & outer))
        def _(side=side):
            co[0, side, 0] = jnp.full((4, 16, 128), float(ROCKS), f32)
            co[0, side, 1] = jnp.zeros((4, 16, 128), f32)

        @pl.when(jnp.logical_not(ok))
        def _(side=side):
            co[1, side, 0] = jnp.full((4, 16, 128), float(ROCKS), f32)
            co[1, side, 1] = jnp.zeros((4, 16, 128), f32)

    well_x, well_y, well_z = wells[0:1, :], wells[1:2, :], wells[2:3, :]
    rate = well_rates[...]
    x0, y0 = NL * xc - LO, NL * gy + LX * core - 4
    columns = depth_of(lax.broadcasted_iota(jnp.int32, (512, WELLS), 0))
    one_z = jnp.where(columns == well_z, 1.0, 0.0).astype(jnp.bfloat16)
    hot_b[:, 0:WELLS] = one_z
    hot_b[:, WELLS:] = one_z
    pair_ids = lax.broadcasted_iota(jnp.int32, (48, WELLS), 0)
    second = pair_ids >= 24
    row_ids = jnp.where(second, pair_ids - 24, pair_ids) + y0
    layer_ids = jnp.where(second, 1, 0) + x0
    high_part = rate.astype(jnp.bfloat16).astype(f32)
    low_part = rate - high_part

    def hot_rows(l, _):
        here = (row_ids == well_y) & (layer_ids == well_x - 2 * l)
        at = pl.ds(pl.multiple_of(48 * l, 16), 48)
        hot_a[at, 0:WELLS] = jnp.where(here, high_part, 0.0).astype(jnp.bfloat16)
        hot_a[at, WELLS:] = jnp.where(here, low_part, 0.0).astype(jnp.bfloat16)
        return 0

    lax.fori_loop(0, (EL + 1) // 2, hot_rows, 0)

    def spread(m, _):
        at = pl.ds(pl.multiple_of(336 * m, 16), 336)
        got = lax.dot_general(
            hot_a[at, :], hot_b[...], (((1,), (1,)), ((), ())), preferred_element_type=f32
        )
        for z in range(4):
            rt[z, pl.ds(14 * m, 14)] = got[:, lanes(z)].reshape(14, 24, 128)
        return 0

    lax.fori_loop(0, 3, spread, 0)

    def table(ref, rule):
        return [rule(jnp.full((8, 128), ref[k], f32)) for k in range(ROCKS)]

    tab_h = table(perm_tab, lambda v: 0.5 / v) + [jnp.full((8, 128), FAR, f32)]
    tab_s = table(poro_tab, lambda v: (COMPRESS * VOLUME) * v) + [jnp.full((8, 128), 1.0, f32)]

    def lookup(kinds, n=8):
        def tall(value):
            return value if n == 8 else jnp.concatenate([value] * (n // 8), axis=0)

        h, s = tall(tab_h[0]), tall(tab_s[0])
        for k in range(1, ROCKS + 1):
            later = kinds > k - 0.5
            h = jnp.where(later, tall(tab_h[k]), h)
            s = jnp.where(later, tall(tab_s[k]), s)
        return h, s

    def unpack_layers(first, last, at_row, tiles=(0, 1, 2)):
        def body(l, _):
            for z in range(4):
                for t in tiles:
                    h, s = lookup(st_r[l, 8 * t : 8 * t + 8, lanes(z)])
                    e = at_row + 8 * t
                    hh[z, l, e : e + 8, :] = h
                    st[z, l, e : e + 8, :] = s
                    pa[z, l, e : e + 8, :] = st_p[l, 8 * t : 8 * t + 8, lanes(z)]
            return 0

        lax.fori_loop(first, last, body, 0)

    for copy in blocks:
        copy.wait()
    arrived(0, st_r.at[pl.ds(LO, LX)])
    arrived(1, st_p.at[pl.ds(LO, LX)])
    by_core(lambda c: unpack_layers(LO, LO + NL, RO - 8 * c))

    def side_faces(l, e0=8, e1=32, n0=0, n1=32):
        for z in range(4):
            te[z, l, e0:e1, :] = recip(hh[z, l, e0:e1, :] + hh[z, l + 1, e0:e1, :])
            tn[z, l, n0:n1, :] = recip(hh[z, l, n0:n1, :] + hh[z, l, n0 + 1 : n1 + 1, :])

    def weights(l, e0=8, e1=32):
        own_h = [hh[z, l, e0:e1, :] for z in range(4)]
        deeper = next_z(own_h)
        below = [recip(own_h[z] + deeper[z]) for z in range(4)]
        last = lax.broadcasted_iota(jnp.int32, (e1 - e0, 128), 1) == 127
        below[3] = jnp.where(last, 0.0, below[3])
        above = prev_z(below)
        for z in (1, 2, 3, 0):
            tb[z, l, e0:e1, :] = below[z]
            storage = st[z, l, e0:e1, :]
            diagonal = (
                storage + te[z, l, e0:e1, :] + te[z, l - 1, e0:e1, :]
                + tn[z, l, e0:e1, :] + tn[z, l, e0 - 1 : e1 - 1, :] + below[z] + above[z]
            )
            ww[z, l, e0:e1, :] = OMEGA * recip(diagonal)
            src[z, l, e0:e1, :] = storage * pa[z, l, e0:e1, :] + rt[z, l, e0 - 8 : e1 - 8, :]

    def one_pass(old, new, start, stop, block, e0=8, e1=32):
        def body(l):
            here = [old[z, l, e0:e1, :] for z in range(4)]
            faces = [tb[z, l, e0:e1, :] for z in range(4)]
            deeper = next_z(here)
            shallower = prev_z([faces[z] * here[z] for z in range(4)])
            for z in (1, 2, 3, 0):
                total = (
                    src[z, l, e0:e1, :] + faces[z] * deeper[z] + shallower[z]
                    + te[z, l, e0:e1, :] * old[z, l + 1, e0:e1, :]
                    + te[z, l - 1, e0:e1, :] * old[z, l - 1, e0:e1, :]
                    + tn[z, l, e0:e1, :] * old[z, l, e0 + 1 : e1 + 1, :]
                    + tn[z, l, e0 - 1 : e1 - 1, :] * old[z, l, e0 - 1 : e1 - 1, :]
                )
                new[z, l, e0:e1, :] = (1.0 - OMEGA) * here[z] + ww[z, l, e0:e1, :] * total

        layers(start, stop, block, body)

    layers(LO, LO + NL - 1, 4, side_faces)
    layers(5, 35, 3, weights)
    one_pass(pa, pb, 5, 35, 3)
    one_pass(pb, pc, 6, 34, 4)

    def fraction(s):
        q = s * s
        return q * recip(1.5 * q + (0.5 - s))

    arrived(2, st_s.at[pl.ds(0, LX)])
    arrived(3, st_b.at[pl.ds(0, LX)])

    def unpack_fraction(c):
        def body(l, _):
            for z in range(4):
                for t in range(3):
                    e = 8 - 8 * c + 8 * t
                    fs[z, l, e : e + 8, :] = fraction(st_s[l, 8 * t : 8 * t + 8, lanes(z)])
            return 0

        lax.fori_loop(0, NL, body, 0)

    by_core(unpack_fraction)

    def unpack_corner(kind, c):
        e4 = 8 if c == kind else 28
        for side, place in ((0, 0), (1, LO + NL)):
            at = pl.ds(place, 4)
            for r in range(4):
                h, s = lookup(co[kind, side, 0, r], 16)
                for z in range(4):
                    hh[z, at, e4 + r, :] = h[4 * z : 4 * z + 4]
                    st[z, at, e4 + r, :] = s[4 * z : 4 * z + 4]
                    pa[z, at, e4 + r, :] = co[kind, side, 1, r, 4 * z : 4 * z + 4, :]

    def unpack_along(c):
        unpack_layers(0, LO, RO - 8 * c, (c, c + 1))
        unpack_layers(LO + NL, EL, RO - 8 * c, (c, c + 1))
        unpack_corner(1, c)

    def unpack_across(c):
        e = 7 if c == 0 else 28
        for z in range(4):
            for r in range(5):
                for g in range(4):
                    at = pl.ds(LO + 8 * g, 8)
                    h, s = lookup(ys_r[r, 8 * g : 8 * g + 8, lanes(z)])
                    hh[z, at, e + r, :] = h
                    st[z, at, e + r, :] = s
                    pa[z, at, e + r, :] = ys_p[r, 8 * g : 8 * g + 8, lanes(z)]
            fs[z, :, 7 if c == 0 else 24, :] = fraction(ys_s[:, lanes(z)])
        unpack_corner(0, c)

    rows_here = pl.ds(pl.multiple_of(8 * core, 8), 16)
    arrived(7, st_r.at[pl.ds(0, 4), rows_here, :], low)
    arrived(8, st_p.at[pl.ds(0, 4), rows_here, :], low)
    arrived(9, st_r.at[pl.ds(LO + NL, 5), rows_here, :], high)
    arrived(10, st_p.at[pl.ds(LO + NL, 5), rows_here, :], high)
    arrived(13, co.at[1, 0], low)
    arrived(14, co.at[1, 1], high)
    by_core(unpack_along)
    arrived(4, ys_r, outer)
    arrived(5, ys_p, outer)
    arrived(6, ys_s, outer)
    arrived(11, co.at[0, 0], low & outer)
    arrived(12, co.at[0, 1], high & outer)
    by_core(unpack_across)

    def finish_passes(c):
        e0, e1 = (8, 16) if c == 0 else (24, 32)
        n0 = 0 if c == 0 else 24
        layers(0, LO, 2, side_faces)
        layers(LO + NL - 1, EL - 1, 2, side_faces)
        layers(LO, LO + NL - 1, 4, lambda l: side_faces(l, e0, e1, n0, e1))
        layers(1, 5, 4, weights)
        layers(35, 40, 5, weights)
        layers(5, 35, 6, lambda l: weights(l, e0, e1))
        one_pass(pa, pb, 1, 5, 4)
        one_pass(pa, pb, 35, 40, 5)
        one_pass(pa, pb, 5, 35, 6, e0, e1)
        one_pass(pb, pc, 2, 6, 4)
        one_pass(pb, pc, 34, 39, 5)
        one_pass(pb, pc, 6, 34, 7, e0, e1)

    by_core(finish_passes)
    one_pass(pc, pd, 3, 38, 4)
    one_pass(pd, pa, 4, 37, 4)

    def fluxes(l):
        e = l + LO
        center = [pa[z, e, RO : RO + 16, :] for z in range(4)]
        frac = [fs[z, l, 8:24, :] for z in range(4)]
        deeper, frac_deep = next_z(center), next_z(frac)
        drained = []
        for z in range(4):
            flow = tb[z, e, RO : RO + 16, :] * (center[z] - deeper[z])
            drained.append(flow * jnp.where(flow > 0, frac[z], frac_deep[z]))
        entered = prev_z(drained)
        at = pl.ds(pl.multiple_of(8 * core, 8), 16)
        for z in range(4):
            p, f = center[z], frac[z]
            res_p[l, :, lanes(z)] = p
            through = jnp.maximum(
                st_b[l, :, lanes(z)] + te[z, e, RO : RO + 16, :] * (p - pa[z, e + 1, RO : RO + 16, :]), 0.0
            )
            north = tn[z, e, RO : RO + 16, :] * (p - pa[z, e, RO + 1 : RO + 17, :])
            south = tn[z, e, RO - 1 : RO + 15, :] * (p - pa[z, e, RO - 1 : RO + 15, :])
            leaving = drained[z] - entered[z]
            leaving = leaving + north * jnp.where(north > 0, f, fs[z, l, 9:25, :])
            leaving = leaving + south * jnp.where(south > 0, f, fs[z, l, 7:23, :])
            rates = rt[z, e, 4:20, :]
            extra = rates * jnp.where(rates > 0, 1.0, f) - leaving
            per_volume = recip((1.0 / COMPRESS) * st[z, e, RO : RO + 16, :])
            s = st_s[l, at, lanes(z)]
            q = s * s
            inverse = recip(1.5 * q + (0.5 - s))
            slope = (s - q) * inverse * inverse
            extra = extra * per_volume
            relative = through * per_volume
            step = recip(1.0 + relative * slope)
            hh[z, l, 8:24, :] = s + extra
            hh[z, l, 24:40, :] = per_volume
            pc[z, l, 8:24, :] = s + (extra - relative * f) * step
            pc[z, l, 24:40, :] = per_volume * step
            ww[z, l, 8:24, :] = relative
            ww[z, l, 24:40, :] = through

    layers(0, NL, 2, fluxes)

    theirs = pl.ds(LX * (1 - core), LX)
    out_rows = pl.ds(pl.multiple_of(16 * core, 16), 16)
    keep_p = local(8, res_p.at[own0], out_p.at[:, out_rows, :])
    give_p = remote(18, 15, res_p.at[theirs], out_p.at[:, out_rows, :], partner)

    def restore(ref, first, count):
        at = pl.ds(first, count)
        value = ref[at].reshape(16 * count, 512)
        ref[at] = permuted(value, back[...], 3).reshape(count, 16, 512)

    def hand_back_pressure():
        for first in (0, 16):
            restore(res_p, first, 16)
        keep_p.start()
        give_p.start()

    pl.when(low)(hand_back_pressure)

    def newton(s, c, relative):
        q = s * s
        d = 1.5 * q + (0.5 - s)
        return d * d + relative * (s - q), d * (d * (s - c) + relative * q)

    waves, keeps, gives = [], [], []
    for half in (0, 1):
        tiles = (2 * half, 2 * half + 1)
        wide = pl.ds(256 * half, 256)
        waves.append(remote(19 + half, 16 + half, face_out.at[half], face_in.at[half], (gx + 2, gy)))
        keeps.append(local(10 + half, res_s.at[own0, :, wide], out_s.at[:, out_rows, wide]))
        gives.append(remote(21 + half, 18 + half, res_s.at[theirs, :, wide], out_s.at[:, out_rows, wide], partner))

        @pl.when(jnp.logical_not(low))
        def _(half=half, tiles=tiles):
            for z in tiles:
                face_in[half, z % 2] = st_b[0, :, lanes(z)]

        arrived(16 + half, face_in.at[half], low)

        def sweep(l, coming, tiles=tiles):
            going = []
            for z in tiles:
                relative = ww[z, l, 8:24, :]
                inflow = coming[z % 2]
                c = hh[z, l, 8:24, :] + hh[z, l, 24:40, :] * inflow
                s = jnp.clip(pc[z, l, 8:24, :] + pc[z, l, 24:40, :] * inflow, 0.0, 1.0)
                below, above = newton(s, c, relative)
                s = jnp.clip(s - above * recip(below), 0.0, 1.0)
                below, above = newton(s, c, relative)
                top = jnp.minimum(jnp.maximum(s * below - above, 0.0), below)
                res_s[l, :, lanes(z)] = top * recip(below)
                rest = (below - top) * (MOBILITY**0.5)
                top = top * top
                going.append(ww[z, l, 24:40, :] * top * recip(top + rest * rest))
            return going

        coming = lax.fori_loop(0, NL, sweep, [face_in[half, 0], face_in[half, 1]], unroll=4)
        for z in (0, 1):
            face_out[half, z] = coming[z]
        pl.when(high)(waves[half].start)
        keeps[half].start()
        gives[half].start()

    pl.when(jnp.logical_not(low))(hand_back_pressure)

    for ok, copy in sends + sends_late:
        guarded(ok, copy.wait_send)
    keep_p.wait()
    give_p.wait()
    for half in (0, 1):
        keeps[half].wait()
        pl.when(high)(waves[half].wait_send)
        gives[half].wait()


def finish_kernel(p_in, s_in, p_out, s_out, held_p, held, back, sem):
    parts, plain = [], []
    for i in range(4):
        at = pl.ds(4 * i, 4)
        parts.append((
            pltpu.make_async_copy(s_in.at[at], held.at[at], sem.at[i]),
            pltpu.make_async_copy(held.at[at], s_out.at[at], sem.at[4 + i]),
        ))
        plain.append((
            pltpu.make_async_copy(p_in.at[at], held_p.at[at], sem.at[8 + i]),
            pltpu.make_async_copy(held_p.at[at], p_out.at[at], sem.at[12 + i]),
        ))
        parts[i][0].start()
    for i in range(4):
        plain[i][0].start()
    ahead = lax.broadcasted_iota(jnp.int32, (512, 512), 0)
    aside = lax.broadcasted_iota(jnp.int32, (512, 512), 1)
    back[...] = jnp.where(4 * lax.rem(ahead, 128) + ahead // 128 == aside, 1.0, 0.0).astype(jnp.bfloat16)
    for i in range(4):
        parts[i][0].wait()
        at = pl.ds(4 * i, 4)
        value = held[at].reshape(128, 512)
        held[at] = permuted(value, back[...], 3).reshape(4, 32, 512)
        parts[i][1].start()
        plain[i][0].wait()
        plain[i][1].start()
    for i in range(4):
        parts[i][1].wait()
        plain[i][1].wait()


def shards(rock, perm_tab, poro_tab, base, press, sat0, wells, well_rates):
    f32, i32 = jnp.float32, jnp.int32
    shape = jax.ShapeDtypeStruct(rock.shape, f32)
    hbm = pl.BlockSpec(memory_space=pl.ANY)
    smem = pl.BlockSpec(memory_space=pltpu.SMEM)
    vmem = pl.BlockSpec(memory_space=pltpu.VMEM)
    extended = pltpu.VMEM((4, EL, ER, 128), f32)
    block = pltpu.VMEM((LX, 32, 512), f32)
    halfway = pl.pallas_call(
        step_kernel,
        out_shape=(shape, shape),
        in_specs=[hbm, smem, smem, hbm, hbm, hbm, vmem, vmem],
        out_specs=(hbm, hbm),
        scratch_shapes=[
            pltpu.VMEM((EL, 24, 512), f32),
            pltpu.VMEM((EL, 24, 512), f32),
            pltpu.VMEM((NL, 24, 512), f32),
            pltpu.VMEM((NL, 16, 512), f32),
            pltpu.VMEM((LX, 32, 512), i32),
            block, block, block, block,
            pltpu.VMEM((2, 5, LX, 512), f32),
            pltpu.VMEM((2, 5, LX, 512), f32),
            pltpu.VMEM((2, LX, 512), f32),
            pltpu.VMEM((4, 2, 4, 16, 128), f32),
            pltpu.VMEM((5, NL, 512), f32),
            pltpu.VMEM((5, NL, 512), f32),
            pltpu.VMEM((NL, 512), f32),
            pltpu.VMEM((2, 2, 2, 4, 16, 128), f32),
            extended, extended, extended, extended, extended, extended,
            extended, extended, extended, extended, extended,
            pltpu.VMEM((4, EL + 1, 24, 128), f32),
            pltpu.VMEM((24 * (EL + 1), 2 * WELLS), jnp.bfloat16),
            pltpu.VMEM((512, 2 * WELLS), jnp.bfloat16),
            pltpu.VMEM((4, NL, 32, 128), f32),
            pltpu.VMEM((512, 512), jnp.bfloat16),
            pltpu.VMEM((512, 512), jnp.bfloat16),
            pltpu.VMEM((2, 2, 16, 128), f32),
            pltpu.VMEM((2, 2, 16, 128), f32),
            pltpu.VMEM((NL, 16, 512), f32),
            pltpu.VMEM((NL, 16, 512), f32),
            pltpu.SemaphoreType.DMA((12,)),
            pltpu.SemaphoreType.DMA((23,)),
            pltpu.SemaphoreType.DMA((20,)),
        ],
        compiler_params=pltpu.CompilerParams(
            collective_id=0, has_side_effects=True, vmem_limit_bytes=60 * 1024 * 1024
        ),
    )(rock, perm_tab, poro_tab, base, press, sat0, wells, well_rates.reshape(1, WELLS))
    return pl.pallas_call(
        finish_kernel,
        out_shape=(shape, shape),
        in_specs=[hbm, hbm],
        out_specs=(hbm, hbm),
        scratch_shapes=[block, block, pltpu.VMEM((512, 512), jnp.bfloat16), pltpu.SemaphoreType.DMA((32,))],
        compiler_params=pltpu.CompilerParams(vmem_limit_bytes=60 * 1024 * 1024),
    )(*halfway)


def solution(mesh):
    block = P("gx", "gy", None)
    return jax.shard_map(
        shards,
        mesh=mesh,
        in_specs=(block, P(), P(), block, block, block, P(), P()),
        out_specs=(block, block),
        check_vma=False,
    )
```
